1024 devices in a mesh: dp: 32 (over x_lo, y, core), expert: 32 (over x_hi, z).
Axes of the slice: x: 4 (x_hi: 2, x_lo: 2; x = x_hi * 2 + x_lo), y: 8, z: 16, core: 2. Of those that a mesh axis runs over, the one named last changes fastest.
Arguments:
- tokens: bfloat16 [2048, 4096], P('expert', 'dp'), may hold values from -6 to 6
- grad_out: bfloat16 [2048, 4096], P('expert', 'dp'), may hold values from -6 to 6
- routes: int32 [2048, 8], P('expert'), may hold values from 0 to 31, all different within a row; in each aligned block of 64 rows (0 to 63, 64 to 127, ...) at most 24 rows name the same one
- gate_probs: float32 [2048, 8], P('expert'), may hold values from 0.03 to 0.6
- w_gate: bfloat16 [32, 4096, 768], P('expert', 'dp'), may hold values from -0.09375 to 0.09375
- w_up: bfloat16 [32, 4096, 768], P('expert', 'dp'), may hold values from -0.09375 to 0.09375
- w_down: bfloat16 [32, 768, 4096], P('expert', None, 'dp'), may hold values from -0.21875 to 0.21875
- dest: int32 [32], P('expert'), may hold values from 0 to 31, as said below
- next_master: float32 [32, 384, 2048], P('expert', 'dp'), may hold values from -3 to 3
- next_first: float32 [32, 384, 2048], P('expert', 'dp'), may hold values from -3 to 3
- next_second: float32 [32, 384, 2048], P('expert', 'dp'), may hold values from 0.01 to 1
Outputs:
- mixed: bfloat16 [2048, 4096], P('expert', 'dp')
- token_grad: bfloat16 [2048, 4096], P('expert', 'dp')
- grad_gate: bfloat16 [32, 4096, 768], P('expert', 'dp')
- grad_up: bfloat16 [32, 4096, 768], P('expert', 'dp')
- grad_down: bfloat16 [32, 768, 4096], P('expert', None, 'dp')
- moved_master: float32 [32, 384, 2048], P('expert', 'dp')
- moved_first: float32 [32, 384, 2048], P('expert', 'dp')
- moved_second: float32 [32, 384, 2048], P('expert', 'dp')
The draws below stay inside these ranges and needn't reach their ends.
Inputs may be any that keep to these rules, and one draw needn't show every extreme that they name: `routes`: among the 64 tokens of one group, no expert is named more than 24 times, a bound that some block reaches. `dest`: each entry is its own index or its index plus 32//2 modulo 32, and an entry and its partner's entry name each other.
All inputs are finite; a program needn't handle non-finite values.
Results may differ from the reference program's by a relative error of at most 0.0064.
Values may be sent and summed in bfloat16 or wider, within the bound.
No kernel may reach another device: no remote copies, remote signals or barrier semaphores. Data moves between devices by JAX's collectives and lax.ppermute only.
A program may use at most 64 MiB of HBM per device.

```python
import math
import jax
import jax.numpy as jnp
import numpy as np
from jax import lax

D = 4096
FF = 768
TOP = 8
TOK_GRP = 64
EXPERTS = 32
TOKENS = 2048
CAP = 24
NEXT_FF = 384
NEXT_D = 2048
N_EXPERT = 32


def draw_dest(key, part):
    key = jax.random.fold_in(key, 7)
    halfway = N_EXPERT // 2
    moving = jax.random.randint(key, (halfway,), 0, 2).astype(jnp.int32)
    paired = jnp.concatenate([moving, moving])
    positions = jnp.arange(N_EXPERT, dtype=jnp.int32)
    partner = (positions + halfway) % N_EXPERT
    return jnp.where(paired == 1, partner, positions).astype(jnp.int32)


def block_levels(key, shape, shards, low, largest):
    factor_of, own = 1.0, jax.random.fold_in(key, 6)
    for dim, shards_of in shards:
        steps = jnp.exp(jax.random.uniform(jax.random.fold_in(own, dim), (shards_of,), jnp.float32, low / len(shards), largest / len(shards)))
        factor_of = factor_of * jnp.repeat(steps, shape[dim] // shards_of).reshape([-1 if axis == dim else 1 for axis in range(len(shape))])
    return factor_of


def shared_out(rng, own, number, rows, number_of, top, reach, lean):
    ranking = jax.random.permutation(rng, number_of)
    heavy_load, ordinary = portions_of(number_of, rows * top, reach, lean, True), portions_of(number_of, rows * top, reach, lean, False)
    places = jnp.arange(number_of)

    def named(lengths, offset_by):
        used = int((lengths > 0).sum())
        fixed = max(1, used // 4)
        shifted = fixed + (places - fixed + offset_by * (used - fixed)) % max(1, number_of - fixed)
        return jnp.zeros((number_of,), jnp.int32).at[ranking[jnp.where(places < fixed, places, shifted)]].set(jnp.asarray(lengths, jnp.int32))

    lengths = jnp.where(number % 4 == 0, named(heavy_load, number // 4), named(ordinary, number - number // 4 - 1))
    mixed = jax.random.permutation(jax.random.fold_in(own, 3), number_of)
    source_of, sink = mixed[0:number_of // 2 * 2:2], mixed[1:number_of // 2 * 2:2]
    slack = jnp.minimum(lengths[source_of] - 1, reach - lengths[sink]) // 2
    slack = jnp.where((source_of == ranking[0]) | (sink == ranking[0]) | (lengths[sink] == 0), 0, jnp.maximum(slack, 0))
    shifted = jax.random.randint(jax.random.fold_in(own, 4), (number_of // 2,), 0, 1 << 20) % (slack + 1)
    lengths = lengths.at[source_of].add(-shifted).at[sink].add(shifted)
    labels = jnp.searchsorted(jnp.cumsum(lengths), jnp.arange(rows * top), side="right").astype(jnp.int32)
    listing = labels.reshape(top, rows).T
    listing = listing[jax.random.permutation(jax.random.fold_in(own, 1), rows)]
    offset_by = jax.random.randint(jax.random.fold_in(own, 2), (rows, 1), 0, top)
    return jnp.take_along_axis(listing, (jnp.arange(top)[None, :] + offset_by) % top, axis=1)


def portions_of(number_of, total, reach, skew, full):
    portions = [(1 << 20) // math.isqrt(grade ** skew) + 1 for grade in range(1, number_of + 1)]
    largest = reach if full else min(reach, max(-(-total // number_of), total * portions[0] // sum(portions)))
    least = 1 if total - largest >= number_of - 1 else 0
    counts, spare = [largest] + [least] * (number_of - 1), total - largest - least * (number_of - 1)
    while spare > 0:
        candidates = [i for i in range(1, number_of) if counts[i] < largest] or [i for i in range(1, number_of) if counts[i] < reach]
        whole, left = sum([portions[i] for i in candidates]), spare
        for i in candidates:
            addition = min(reach - counts[i], max(1, left * portions[i] // whole), spare)
            counts[i] = counts[i] + addition
            spare = spare - addition
    return np.array(counts)


def scatter_about(stream_key, dims, deviation, bound, cuts=(), kind=jnp.bfloat16):
    loudness = block_levels(stream_key, dims, cuts, -0.22, 0.18) if cuts else 1.0
    result = jax.random.normal(stream_key, dims, jnp.float32) * deviation * loudness
    return jnp.minimum(jnp.maximum(result, -bound), bound).astype(kind)


def setup_inputs(seed: int = 0) -> dict:
    key_of = jax.random.split(jax.random.key(seed), 12)
    tokens = scatter_about(key_of[0], (TOKENS, D), 1.0, 6.0, ((0, 32), (1, 32)))
    grad_out = scatter_about(key_of[1], (TOKENS, D), 1.0, 6.0, ((0, 32), (1, 32)))
    routes_keys = jax.random.split(jax.random.fold_in(key_of[2], 1), TOKENS // TOK_GRP)
    routes_turns = jax.random.permutation(jax.random.fold_in(key_of[2], 3), TOKENS // TOK_GRP)
    routes = jax.vmap(lambda own, number: shared_out(jax.random.fold_in(key_of[2], 2), own, number, TOK_GRP, EXPERTS, TOP, CAP, 2))(routes_keys, routes_turns).reshape((TOKENS, TOP))
    gate_probs = jnp.clip(jnp.exp(math.log(0.6) - 2.9957323 * jax.random.uniform(key_of[3], (TOKENS, TOP), jnp.float32) ** block_levels(key_of[3], (TOKENS, TOP), ((0, 32),), -0.2, 0.2)), 0.03, 0.6)
    w_gate = scatter_about(key_of[4], (EXPERTS, D, FF), D ** -0.5, 0.09375, ((0, 32), (1, 32)))
    w_up = scatter_about(key_of[5], (EXPERTS, D, FF), D ** -0.5, 0.09375, ((0, 32), (1, 32)))
    w_down = scatter_about(key_of[6], (EXPERTS, FF, D), FF ** -0.5, 0.21875, ((0, 32), (2, 32)))
    dest = draw_dest(jax.random.fold_in(key_of[11], 71), 0)
    next_master = scatter_about(key_of[8], (N_EXPERT, NEXT_FF, NEXT_D), 0.5, 3.0, ((0, 32), (1, 32)), jnp.float32)
    next_first = scatter_about(key_of[9], (N_EXPERT, NEXT_FF, NEXT_D), 0.5, 3.0, ((0, 32), (1, 32)), jnp.float32)
    next_second = jnp.clip(jnp.exp(math.log(1.0) - 4.6051702 * jax.random.uniform(key_of[10], (N_EXPERT, NEXT_FF, NEXT_D), jnp.float32) ** block_levels(key_of[10], (N_EXPERT, NEXT_FF, NEXT_D), ((0, 32), (1, 32)), -0.2, 0.2)), 0.01, 1.0)
    return {"tokens": tokens, "grad_out": grad_out, "routes": routes, "gate_probs": gate_probs, "w_gate": w_gate, "w_up": w_up, "w_down": w_down, "dest": dest, "next_master": next_master, "next_first": next_first, "next_second": next_second}


def slot_table(route_rows, expert_count, capacity):
    flat_ids = route_rows.reshape(-1)
    onehot = (flat_ids[:, None] == jnp.arange(expert_count, dtype=jnp.int32)[None, :]).astype(jnp.int32)
    earlier = jnp.cumsum(onehot, axis=0) - onehot
    position = jnp.sum(earlier * onehot, axis=1).astype(jnp.int32)
    slot_ids = flat_ids * capacity + position
    return (slot_ids[:, None] == jnp.arange(expert_count * capacity, dtype=jnp.int32)[None, :]).astype(jnp.float32)


def reference(tokens, grad_out, routes, gate_probs, w_gate, w_up, w_down, dest, next_master, next_first, next_second):
    groups = N_EXPERT
    capacity = CAP
    slot_rows = groups * capacity
    assigned = TOK_GRP * TOP
    tok_groups = tokens.reshape(groups, TOK_GRP, D)
    cot_groups = grad_out.reshape(groups, TOK_GRP, D)
    route_groups = routes.reshape(groups, TOK_GRP, TOP)
    prob_groups = gate_probs.reshape(groups, assigned)
    tables = jax.vmap(lambda rows: slot_table(rows, EXPERTS, capacity))(route_groups)
    x_assign = jnp.repeat(tok_groups, TOP, axis=1).astype(jnp.float32)
    dy_assign = (prob_groups[..., None] * jnp.repeat(cot_groups, TOP, axis=1).astype(jnp.float32)).astype(jnp.bfloat16)
    x_slots = jnp.einsum('gas,gad->gsd', tables, x_assign).astype(jnp.bfloat16)
    dy_slots = jnp.einsum('gas,gad->gsd', tables, dy_assign.astype(jnp.float32)).astype(jnp.bfloat16)

    def to_experts(slots):
        return slots.reshape(groups, EXPERTS, capacity, D).transpose(1, 0, 2, 3).reshape(EXPERTS, slot_rows, D)

    def expert_work(operands):
        x_expert, dy_expert, wg_expert, wu_expert, wd_expert = operands
        gate = jnp.dot(x_expert, wg_expert, preferred_element_type=jnp.float32)
        up_val = jnp.dot(x_expert, wu_expert, preferred_element_type=jnp.float32)
        back = jnp.dot(dy_expert, wd_expert.T, preferred_element_type=jnp.float32)
        sigma_val = jax.nn.sigmoid(gate)
        act = (gate * sigma_val * up_val).astype(jnp.bfloat16)
        grad_g = (back * up_val * sigma_val * (1.0 + gate * (1.0 - sigma_val))).astype(jnp.bfloat16)
        grad_u = (back * gate * sigma_val).astype(jnp.bfloat16)
        slot_y = jnp.dot(act, wd_expert, preferred_element_type=jnp.float32).astype(jnp.bfloat16)
        slot_dx = (jnp.dot(grad_g, wg_expert.T, preferred_element_type=jnp.float32)
                   + jnp.dot(grad_u, wu_expert.T, preferred_element_type=jnp.float32)).astype(jnp.bfloat16)
        dwg = jnp.dot(x_expert.T, grad_g, preferred_element_type=jnp.float32).astype(jnp.bfloat16)
        dwu = jnp.dot(x_expert.T, grad_u, preferred_element_type=jnp.float32).astype(jnp.bfloat16)
        dwd = jnp.dot(act.T, dy_expert, preferred_element_type=jnp.float32).astype(jnp.bfloat16)
        return slot_y, slot_dx, dwg, dwu, dwd

    slot_y, slot_dx, grad_gate, grad_up, grad_down = lax.map(
        expert_work, (to_experts(x_slots), to_experts(dy_slots), w_gate, w_up, w_down))

    def to_groups(values):
        return values.reshape(EXPERTS, groups, capacity, D).transpose(1, 0, 2, 3).reshape(groups, EXPERTS * capacity, D)

    y_assign = jnp.einsum('gas,gsd->gad', tables, to_groups(slot_y).astype(jnp.float32))
    dx_assign = jnp.einsum('gas,gsd->gad', tables, to_groups(slot_dx).astype(jnp.float32))
    mixed = jnp.sum((prob_groups[..., None] * y_assign).reshape(groups, TOK_GRP, TOP, D), axis=2)
    token_grad = jnp.sum(dx_assign.reshape(groups, TOK_GRP, TOP, D), axis=2)
    mixed = mixed.reshape(TOKENS, D).astype(jnp.bfloat16)
    token_grad = token_grad.reshape(TOKENS, D).astype(jnp.bfloat16)
    moved_master = jnp.take(next_master, dest, axis=0)
    moved_first = jnp.take(next_first, dest, axis=0)
    moved_second = jnp.take(next_second, dest, axis=0)
    return (mixed, token_grad, grad_gate, grad_up, grad_down, moved_master, moved_first, moved_second)
```

```python
import functools

import jax
import jax.numpy as jnp
from jax import lax
from jax.experimental import pallas as pl
from jax.experimental.pallas import tpu as pltpu
from jax.sharding import Mesh
from jax.sharding import PartitionSpec as P

EXPERT = ("x_hi", "z")
DP = ("x_lo", "y", "core")
QUAD = ("x_lo", "core")
F32 = jnp.float32
BF16 = jnp.bfloat16
SWAP = [(0, 1), (1, 0)]

TOK = 64
TOP = 8
GROUPS = 32
PART = 6
QUADS = 4
ROWS = GROUPS * PART
WIDE = GROUPS * PART * QUADS
BLK = 128
FF = 768
Y = 8

PARAMS = pltpu.CompilerParams(vmem_limit_bytes=48 * 1024 * 1024)


def call(kernel, out_shape, operands, flops=0, moved=0):
    vmem = pl.BlockSpec(memory_space=pltpu.VMEM)
    smem = pl.BlockSpec(memory_space=pltpu.SMEM)
    return pl.pallas_call(
        kernel,
        out_shape=out_shape,
        in_specs=[smem if o.dtype == jnp.int32 and o.size == 1 else vmem for o in operands],
        out_specs=jax.tree.map(lambda _: vmem, out_shape),
        compiler_params=PARAMS,
        cost_estimate=pl.CostEstimate(flops=flops, bytes_accessed=moved, transcendentals=0),
    )(*operands)


def row_fields(shape, dim):
    r = lax.broadcasted_iota(jnp.int32, shape, dim)
    pair = (r * 2731) >> 16
    rest = r - pair * (QUADS * PART)
    member = (rest * 43) >> 8
    return pair, member, rest - member * PART


def three(value):
    hi = value.astype(BF16)
    left = value - hi.astype(F32)
    mid = left.astype(BF16)
    return hi, mid, (left - mid.astype(F32)).astype(BF16)


def dot(a, b, dims):
    return lax.dot_general(a, b, (dims, ((), ())), preferred_element_type=F32)


def dispatch_kernel(q_ref, routes_ref, probs_ref, near_ref, far_ref, pay_ref, mask_ref, prob_ref):
    q = q_ref[0]
    shape = (TOK, WIDE)
    pair, member, slot = row_fields(shape, 1)
    chosen = jnp.zeros(shape, F32)
    weight = jnp.zeros(shape, F32)
    for k in range(TOP):
        hit = routes_ref[:, k : k + 1] == pair
        chosen = jnp.where(hit, 1.0, chosen)
        weight = jnp.where(hit, probs_ref[:, k : k + 1], weight)
    row = lax.broadcasted_iota(jnp.int32, (TOK, TOK), 0)
    col = lax.broadcasted_iota(jnp.int32, (TOK, TOK), 1)
    before = jnp.where(col < row, 1.0, 0.0).astype(BF16)
    position = dot(before, chosen.astype(BF16), ((1,), (0,)))
    here = (chosen > 0.5) & (position == (q * PART + slot).astype(F32))
    mask = jnp.where(here, 1.0, 0.0)
    prob = jnp.where(here, weight, 0.0)
    mask_ref[...] = mask.astype(BF16)
    prob_ref[...] = prob
    masks = [jnp.where(member == d, mask, 0.0).astype(BF16) for d in range(QUADS)]
    parts = three(prob)
    x = jnp.zeros((WIDE, BLK), F32)
    dy = jnp.zeros((WIDE, BLK), F32)
    zero = jnp.zeros(shape, BF16)
    for d in range(QUADS):
        source = near_ref if d < 2 else far_ref
        lo = (d % 2) * TOK
        x_tok = source[lo : lo + TOK, :BLK]
        dy_tok = source[lo : lo + TOK, BLK:]
        x = x + dot(masks[d], x_tok, ((0,), (0,)))
        for part in parts:
            dy = dy + dot(jnp.where(member == d, part, zero), dy_tok, ((0,), (0,)))
    pay_ref[:, :BLK] = x.astype(BF16)
    pay_ref[:, BLK:] = dy.astype(BF16)


def place(d):
    i = lax.broadcasted_iota(jnp.int32, (ROWS, WIDE), 0)
    r = lax.broadcasted_iota(jnp.int32, (ROWS, WIDE), 1)
    group = (i * 10923) >> 16
    want = group * (QUADS * PART) + d * PART + (i - group * PART)
    return jnp.where(r == want, 1.0, 0.0).astype(BF16)


def partial_kernel(pay_ref, w0, w1, w2, w3, sums_ref, x_ref, dy_ref):
    got = pay_ref[...]
    for d in range(QUADS):
        moved = dot(place(d), got, ((1,), (0,))).astype(BF16)
        x_ref[:, d * BLK : (d + 1) * BLK] = moved[:, :BLK]
        dy_ref[:, d * BLK : (d + 1) * BLK] = moved[:, BLK:]
    for k in range(3):
        rows_ref = dy_ref if k == 2 else x_ref
        total = jnp.zeros((ROWS, FF), F32)
        for d, w in enumerate((w0, w1, w2, w3)):
            total = total + dot(rows_ref[:, d * BLK : (d + 1) * BLK], w[k], ((1,), (0,)))
        sums_ref[:, k * FF : (k + 1) * FF] = total.astype(BF16)


def act_kernel(in_ref, out_ref):
    rows = ROWS // Y
    for lo in range(0, FF, 256):
        vals = []
        for k in range(3):
            block = in_ref[:, k * FF + lo : k * FF + lo + 256].astype(F32)
            total = block[:rows]
            for y in range(1, Y):
                total = total + block[y * rows : (y + 1) * rows]
            vals.append(total)
        gate, up, back = vals
        s = jax.nn.sigmoid(gate)
        out_ref[:, lo : lo + 256] = (gate * s * up).astype(BF16)
        out_ref[:, FF + lo : FF + lo + 256] = (
            back * up * s * (1.0 + gate * (1.0 - s))
        ).astype(BF16)
        out_ref[:, 2 * FF + lo : 2 * FF + lo + 256] = (back * gate * s).astype(BF16)


def back_kernel(h_ref, w0, w1, w2, w3, pay_ref):
    act = h_ref[:, :FF]
    grad_g = h_ref[:, FF : 2 * FF]
    grad_u = h_ref[:, 2 * FF :]
    total = jnp.zeros((WIDE, 2 * BLK), F32)
    for d, w in enumerate((w0, w1, w2, w3)):
        y = dot(act, w[2], ((1,), (1,)))
        dx = dot(grad_g, w[0], ((1,), (1,))) + dot(grad_u, w[1], ((1,), (1,)))
        both = jnp.concatenate([y.astype(BF16), dx.astype(BF16)], axis=1)
        total = total + dot(place(d), both, ((0,), (0,)))
    pay_ref[...] = total.astype(BF16)


def grad_kernel(h_ref, x_ref, dy_ref, keep_ref, send_ref):
    for d in range(QUADS):
        for k in range(3):
            rows_ref = dy_ref if k == 2 else x_ref
            h_at = (FF, 2 * FF, 0)[k]
            part = dot(
                rows_ref[:, d * BLK : (d + 1) * BLK], h_ref[:, h_at : h_at + FF], ((0,), (0,))
            )
            if d % 2:
                send_ref[d // 2, k] = part.astype(BF16)
            else:
                keep_ref[d // 2, k] = part


def combine_kernel(q_ref, pay_ref, mask_ref, prob_ref, out_ref):
    q = q_ref[0]
    shape = (TOK, WIDE)
    _, member, _ = row_fields(shape, 1)
    y = pay_ref[:, :BLK]
    dx = pay_ref[:, BLK:]
    mask = mask_ref[...].astype(F32)
    prob = prob_ref[...]
    for d in range(QUADS):
        at = member == d
        mixed = jnp.zeros((TOK, BLK), F32)
        for part in three(jnp.where(at, prob, 0.0)):
            mixed = mixed + dot(part, y, ((1,), (0,)))
        grad = dot(jnp.where(at, mask, 0.0).astype(BF16), dx, ((1,), (0,)))
        out_ref[q ^ d] = jnp.concatenate([mixed, grad], axis=1).astype(BF16)


def shape_of(*dims, dtype=BF16):
    return jax.ShapeDtypeStruct(dims, dtype)


def shards(
    tokens,
    grad_out,
    routes,
    gate_probs,
    w_gate,
    w_up,
    w_down,
    dest,
    next_master,
    next_first,
    next_second,
):
    quad = (lax.axis_index("x_lo") * 2 + lax.axis_index("core")).astype(jnp.int32).reshape(1)

    with jax.named_scope("tokens_to_quad"):
        mine = jnp.concatenate([tokens, grad_out], axis=1)
        near = jnp.concatenate([mine, lax.ppermute(mine, "core", SWAP)], axis=0)
        far = lax.ppermute(near, "x_lo", SWAP)

    with jax.named_scope("weights_to_quad"):
        w0 = jnp.stack([w_gate[0], w_up[0], w_down[0].T])
        w2 = lax.ppermute(w0, "x_lo", SWAP)
        w1 = lax.ppermute(w0, "core", SWAP)
        w3 = lax.ppermute(w2, "core", SWAP)

    with jax.named_scope("dispatch"):
        pay, mask, prob = call(
            dispatch_kernel,
            (shape_of(WIDE, 2 * BLK), shape_of(TOK, WIDE), shape_of(TOK, WIDE, dtype=F32)),
            (quad, routes, gate_probs, near, far),
            flops=2 * 16 * TOK * WIDE * BLK,
            moved=800000,
        )
        got = lax.all_to_all(pay, EXPERT, split_axis=0, concat_axis=0, tiled=True)

    with jax.named_scope("partial_sums"):
        sums, x_rows, dy_rows = call(
            partial_kernel,
            (shape_of(ROWS, 3 * FF), shape_of(ROWS, 4 * BLK), shape_of(ROWS, 4 * BLK)),
            (got, w0, w1, w2, w3),
            flops=2 * 3 * ROWS * FF * 4 * BLK,
            moved=4000000,
        )
        parts = lax.all_to_all(sums, "y", split_axis=0, concat_axis=0, tiled=True)

    with jax.named_scope("activation"):
        hidden = call(
            act_kernel, shape_of(ROWS // Y, 3 * FF), (parts,), flops=4000000, moved=1000000
        )
        whole = lax.all_gather(hidden, "y", axis=0, tiled=True)

    with jax.named_scope("slot_outputs"):
        back = call(
            back_kernel,
            shape_of(WIDE, 2 * BLK),
            (whole, w0, w1, w2, w3),
            flops=2 * 3 * ROWS * FF * 4 * BLK,
            moved=4000000,
        )
        returned = lax.all_to_all(back, EXPERT, split_axis=0, concat_axis=0, tiled=True)

    with jax.named_scope("weight_grads"):
        keep, send = call(
            grad_kernel,
            (shape_of(2, 3, BLK, FF, dtype=F32), shape_of(2, 3, BLK, FF)),
            (whole, x_rows, dy_rows),
            flops=2 * 3 * ROWS * FF * 4 * BLK,
            moved=6000000,
        )
        pair = keep + lax.ppermute(send, "core", SWAP).astype(F32)
        other = lax.ppermute(pair[1].astype(BF16), "x_lo", SWAP)
        grads = (pair[0] + other.astype(F32)).astype(BF16)

    with jax.named_scope("combine"):
        mixes = call(
            combine_kernel,
            shape_of(QUADS, TOK, 2 * BLK),
            (quad, returned, mask, prob),
            flops=2 * 16 * TOK * WIDE * BLK,
            moved=800000,
        )
        mixes = lax.all_to_all(mixes, QUAD, split_axis=0, concat_axis=0, tiled=True)
        mixes = jnp.sum(mixes.astype(F32), axis=0).astype(BF16)

    with jax.named_scope("relocate"):
        state = jnp.concatenate([next_master, next_first, next_second], axis=0)
        partner = lax.ppermute(state, "x_hi", SWAP)
        place_index = lax.axis_index(EXPERT).astype(jnp.int32)
        moving = dest[0] != place_index
        moved = jnp.where(moving, partner, state)

    return (
        mixes[:, :BLK],
        mixes[:, BLK:],
        grads[0][None],
        grads[1][None],
        grads[2].T[None],
        moved[0:1],
        moved[1:2],
        moved[2:3],
    )


def solution(mesh):
    fine = Mesh(
        mesh.devices.reshape(2, 8, 2, 2, 16), ("x_lo", "y", "core", "x_hi", "z")
    )
    return jax.shard_map(
        shards,
        mesh=fine,
        in_specs=(
            P(EXPERT, DP),
            P(EXPERT, DP),
            P(EXPERT, None),
            P(EXPERT, None),
            P(EXPERT, DP, None),
            P(EXPERT, DP, None),
            P(EXPERT, None, DP),
            P(EXPERT),
            P(EXPERT, DP, None),
            P(EXPERT, DP, None),
            P(EXPERT, DP, None),
        ),
        out_specs=(
            P(EXPERT, DP),
            P(EXPERT, DP),
            P(EXPERT, DP, None),
            P(EXPERT, DP, None),
            P(EXPERT, None, DP),
            P(EXPERT, DP, None),
            P(EXPERT, DP, None),
            P(EXPERT, DP, None),
        ),
        check_vma=False,
    )
```

```python
import functools

import jax
import jax.numpy as jnp
from jax import lax
from jax.experimental import pallas as pl
from jax.experimental.pallas import tpu as pltpu
from jax.sharding import Mesh
from jax.sharding import PartitionSpec as P

EXPERT = ("x_hi", "z")
DP = ("x_lo", "y", "core")
QUAD = ("x_lo", "core")
F32 = jnp.float32
BF16 = jnp.bfloat16
SWAP = [(0, 1), (1, 0)]

TOK = 64
TOP = 8
GROUPS = 32
PART = 6
QUADS = 4
ROWS = GROUPS * PART
WIDE = GROUPS * PART * QUADS
BLK = 128
FF = 768
Y = 8

PARAMS = pltpu.CompilerParams(vmem_limit_bytes=48 * 1024 * 1024)


def call(kernel, out_shape, operands, flops=0, moved=0):
    vmem = pl.BlockSpec(memory_space=pltpu.VMEM)
    smem = pl.BlockSpec(memory_space=pltpu.SMEM)
    return pl.pallas_call(
        kernel,
        out_shape=out_shape,
        in_specs=[smem if o.dtype == jnp.int32 and o.size == 1 else vmem for o in operands],
        out_specs=jax.tree.map(lambda _: vmem, out_shape),
        compiler_params=PARAMS,
        cost_estimate=pl.CostEstimate(flops=flops, bytes_accessed=moved, transcendentals=0),
    )(*operands)


def row_fields(shape, dim):
    r = lax.broadcasted_iota(jnp.int32, shape, dim)
    pair = (r * 2731) >> 16
    rest = r - pair * (QUADS * PART)
    member = (rest * 43) >> 8
    return pair, member, rest - member * PART


def three(value):
    hi = value.astype(BF16)
    left = value - hi.astype(F32)
    mid = left.astype(BF16)
    return hi, mid, (left - mid.astype(F32)).astype(BF16)


def dot(a, b, dims):
    return lax.dot_general(a, b, (dims, ((), ())), preferred_element_type=F32)


def join_kernel(a_ref, b_ref, out_ref):
    out_ref[:, :BLK] = a_ref[...]
    out_ref[:, BLK:] = b_ref[...]


def table_kernel(q_ref, routes_ref, probs_ref, mask_ref, prob_ref):
    q = q_ref[0]
    shape = (TOK, WIDE)
    pair, member, slot = row_fields(shape, 1)
    chosen = jnp.zeros(shape, F32)
    weight = jnp.zeros(shape, F32)
    for k in range(TOP):
        hit = routes_ref[:, k : k + 1] == pair
        chosen = jnp.where(hit, 1.0, chosen)
        weight = jnp.where(hit, probs_ref[:, k : k + 1], weight)
    row = lax.broadcasted_iota(jnp.int32, (TOK, TOK), 0)
    col = lax.broadcasted_iota(jnp.int32, (TOK, TOK), 1)
    before = jnp.where(col < row, 1.0, 0.0).astype(BF16)
    position = dot(before, chosen.astype(BF16), ((1,), (0,)))
    here = (chosen > 0.5) & (position == (q * PART + slot).astype(F32))
    mask = jnp.where(here, 1.0, 0.0)
    prob = jnp.where(here, weight, 0.0)
    mask_ref[...] = mask.astype(BF16)
    prob_ref[...] = prob


def dispatch_kernel(mask_ref, prob_ref, near_ref, far_ref, pay_ref):
    shape = (TOK, WIDE)
    _, member, _ = row_fields(shape, 1)
    mask = mask_ref[...].astype(F32)
    prob = prob_ref[...]
    masks = [jnp.where(member == d, mask, 0.0).astype(BF16) for d in range(QUADS)]
    parts = three(prob)
    x = jnp.zeros((WIDE, BLK), F32)
    dy = jnp.zeros((WIDE, BLK), F32)
    zero = jnp.zeros(shape, BF16)
    for d in range(QUADS):
        source = near_ref if d < 2 else far_ref
        lo = (d % 2) * TOK
        x_tok = source[lo : lo + TOK, :BLK]
        dy_tok = source[lo : lo + TOK, BLK:]
        x = x + dot(masks[d], x_tok, ((0,), (0,)))
        for part in parts:
            dy = dy + dot(jnp.where(member == d, part, zero), dy_tok, ((0,), (0,)))
    pay_ref[:, :BLK] = x.astype(BF16)
    pay_ref[:, BLK:] = dy.astype(BF16)


def place(d):
    i = lax.broadcasted_iota(jnp.int32, (ROWS, WIDE), 0)
    r = lax.broadcasted_iota(jnp.int32, (ROWS, WIDE), 1)
    group = (i * 10923) >> 16
    want = group * (QUADS * PART) + d * PART + (i - group * PART)
    return jnp.where(r == want, 1.0, 0.0).astype(BF16)


def partial_kernel(pay_ref, w0, w1, w2, w3, sums_ref, x_ref, dy_ref):
    got = pay_ref[...]
    for d in range(QUADS):
        moved = dot(place(d), got, ((1,), (0,))).astype(BF16)
        x_ref[:, d * BLK : (d + 1) * BLK] = moved[:, :BLK]
        dy_ref[:, d * BLK : (d + 1) * BLK] = moved[:, BLK:]
    for k in range(3):
        rows_ref = dy_ref if k == 2 else x_ref
        total = jnp.zeros((ROWS, FF), F32)
        for d, w in enumerate((w0, w1, w2, w3)):
            total = total + dot(rows_ref[:, d * BLK : (d + 1) * BLK], w[k], ((1,), (0,)))
        sums_ref[:, k * FF : (k + 1) * FF] = total.astype(BF16)


def act_kernel(in_ref, out_ref):
    rows = ROWS // Y
    for lo in range(0, FF, 256):
        vals = []
        for k in range(3):
            block = in_ref[:, k * FF + lo : k * FF + lo + 256].astype(F32)
            total = block[:rows]
            for y in range(1, Y):
                total = total + block[y * rows : (y + 1) * rows]
            vals.append(total)
        gate, up, back = vals
        s = jax.nn.sigmoid(gate)
        out_ref[:, lo : lo + 256] = (gate * s * up).astype(BF16)
        out_ref[:, FF + lo : FF + lo + 256] = (
            back * up * s * (1.0 + gate * (1.0 - s))
        ).astype(BF16)
        out_ref[:, 2 * FF + lo : 2 * FF + lo + 256] = (back * gate * s).astype(BF16)


def back_kernel(h_ref, w0, w1, w2, w3, pay_ref):
    act = h_ref[:, :FF]
    grad_g = h_ref[:, FF : 2 * FF]
    grad_u = h_ref[:, 2 * FF :]
    total = jnp.zeros((WIDE, 2 * BLK), F32)
    for d, w in enumerate((w0, w1, w2, w3)):
        y = dot(act, w[2], ((1,), (1,)))
        dx = dot(grad_g, w[0], ((1,), (1,))) + dot(grad_u, w[1], ((1,), (1,)))
        both = jnp.concatenate([y.astype(BF16), dx.astype(BF16)], axis=1)
        total = total + dot(place(d), both, ((0,), (0,)))
    pay_ref[...] = total.astype(BF16)


def grad_kernel(h_ref, x_ref, dy_ref, keep_ref, send_ref):
    for d in range(QUADS):
        for k in range(3):
            rows_ref = dy_ref if k == 2 else x_ref
            h_at = (FF, 2 * FF, 0)[k]
            part = dot(
                rows_ref[:, d * BLK : (d + 1) * BLK], h_ref[:, h_at : h_at + FF], ((0,), (0,))
            )
            if d % 2:
                send_ref[d // 2, k] = part.astype(BF16)
            else:
                keep_ref[d // 2, k] = part


def combine_kernel(q_ref, pay_ref, mask_ref, prob_ref, out_ref):
    q = q_ref[0]
    shape = (TOK, WIDE)
    _, member, _ = row_fields(shape, 1)
    y = pay_ref[:, :BLK]
    dx = pay_ref[:, BLK:]
    mask = mask_ref[...].astype(F32)
    prob = prob_ref[...]
    for d in range(QUADS):
        at = member == d
        mixed = jnp.zeros((TOK, BLK), F32)
        for part in three(jnp.where(at, prob, 0.0)):
            mixed = mixed + dot(part, y, ((1,), (0,)))
        grad = dot(jnp.where(at, mask, 0.0).astype(BF16), dx, ((1,), (0,)))
        out_ref[q ^ d] = jnp.concatenate([mixed, grad], axis=1).astype(BF16)


def shape_of(*dims, dtype=BF16):
    return jax.ShapeDtypeStruct(dims, dtype)


def shards(
    tokens,
    grad_out,
    routes,
    gate_probs,
    w_gate,
    w_up,
    w_down,
    dest,
    next_master,
    next_first,
    next_second,
):
    quad = (lax.axis_index("x_lo") * 2 + lax.axis_index("core")).astype(jnp.int32).reshape(1)

    with jax.named_scope("tokens_to_quad"):
        mine = call(join_kernel, shape_of(TOK, 2 * BLK), (tokens, grad_out), moved=65536)
        near = jnp.concatenate([mine, lax.ppermute(mine, "core", SWAP)], axis=0)
        far = lax.ppermute(near, "x_lo", SWAP)

    with jax.named_scope("weights_to_quad"):
        w0 = jnp.stack([w_gate[0], w_up[0], w_down[0].T])
        w2 = lax.ppermute(w0, "x_lo", SWAP)
        w1 = lax.ppermute(w0, "core", SWAP)
        w3 = lax.ppermute(w2, "core", SWAP)

    with jax.named_scope("dispatch"):
        mask, prob = call(
            table_kernel,
            (shape_of(TOK, WIDE), shape_of(TOK, WIDE, dtype=F32)),
            (quad, routes, gate_probs),
            flops=2 * TOK * TOK * WIDE,
            moved=300000,
        )
        pay = call(
            dispatch_kernel,
            shape_of(WIDE, 2 * BLK),
            (mask, prob, near, far),
            flops=2 * 16 * TOK * WIDE * BLK,
            moved=800000,
        )
        got = lax.all_to_all(pay, EXPERT, split_axis=0, concat_axis=0, tiled=True)

    with jax.named_scope("relocate"):
        state = jnp.concatenate([next_master, next_first, next_second], axis=0)

    with jax.named_scope("partial_sums"):
        sums, x_rows, dy_rows = call(
            partial_kernel,
            (shape_of(ROWS, 3 * FF), shape_of(ROWS, 4 * BLK), shape_of(ROWS, 4 * BLK)),
            (got, w0, w1, w2, w3),
            flops=2 * 3 * ROWS * FF * 4 * BLK,
            moved=4000000,
        )
        sums, state = lax.optimization_barrier((sums, state))
        parts = lax.all_to_all(sums, "y", split_axis=0, concat_axis=0, tiled=True)
        partner = lax.ppermute(state, "x_hi", SWAP)
        parts, partner = lax.optimization_barrier((parts, partner))

    with jax.named_scope("activation"):
        hidden = call(
            act_kernel, shape_of(ROWS // Y, 3 * FF), (parts,), flops=4000000, moved=1000000
        )
        whole = lax.all_gather(hidden, "y", axis=0, tiled=True)

    with jax.named_scope("slot_outputs"):
        back = call(
            back_kernel,
            shape_of(WIDE, 2 * BLK),
            (whole, w0, w1, w2, w3),
            flops=2 * 3 * ROWS * FF * 4 * BLK,
            moved=4000000,
        )
        back, whole = lax.optimization_barrier((back, whole))
        returned = lax.all_to_all(back, EXPERT, split_axis=0, concat_axis=0, tiled=True)

    with jax.named_scope("weight_grads"):
        keep, send = call(
            grad_kernel,
            (shape_of(2, 3, BLK, FF, dtype=F32), shape_of(2, 3, BLK, FF)),
            (whole, x_rows, dy_rows),
            flops=2 * 3 * ROWS * FF * 4 * BLK,
            moved=6000000,
        )
        pair = keep + lax.ppermute(send, "core", SWAP).astype(F32)
        other = lax.ppermute(pair[1].astype(BF16), "x_lo", SWAP)
        grads = (pair[0] + other.astype(F32)).astype(BF16)

    with jax.named_scope("combine"):
        mixes = call(
            combine_kernel,
            shape_of(QUADS, TOK, 2 * BLK),
            (quad, returned, mask, prob),
            flops=2 * 16 * TOK * WIDE * BLK,
            moved=800000,
        )
        mixes = lax.all_to_all(mixes, QUAD, split_axis=0, concat_axis=0, tiled=True)
        mixes = jnp.sum(mixes.astype(F32), axis=0).astype(BF16)

    with jax.named_scope("relocate"):
        place_index = lax.axis_index(EXPERT).astype(jnp.int32)
        moving = dest[0] != place_index
        moved = jnp.where(moving, partner, state)

    return (
        mixes[:, :BLK],
        mixes[:, BLK:],
        grads[0][None],
        grads[1][None],
        grads[2].T[None],
        moved[0:1],
        moved[1:2],
        moved[2:3],
    )


def solution(mesh):
    fine = Mesh(
        mesh.devices.reshape(2, 8, 2, 2, 16), ("x_lo", "y", "core", "x_hi", "z")
    )
    return jax.shard_map(
        shards,
        mesh=fine,
        in_specs=(
            P(EXPERT, DP),
            P(EXPERT, DP),
            P(EXPERT, None),
            P(EXPERT, None),
            P(EXPERT, DP, None),
            P(EXPERT, DP, None),
            P(EXPERT, None, DP),
            P(EXPERT),
            P(EXPERT, DP, None),
            P(EXPERT, DP, None),
            P(EXPERT, DP, None),
        ),
        out_specs=(
            P(EXPERT, DP),
            P(EXPERT, DP),
            P(EXPERT, DP, None),
            P(EXPERT, DP, None),
            P(EXPERT, None, DP),
            P(EXPERT, DP, None),
            P(EXPERT, DP, None),
            P(EXPERT, DP, None),
        ),
        check_vma=False,
    )
```

```python
import functools

import jax
import jax.numpy as jnp
from jax import lax
from jax.experimental import pallas as pl
from jax.experimental.pallas import tpu as pltpu
from jax.sharding import Mesh
from jax.sharding import PartitionSpec as P

EXPERT = ("x_hi", "z")
DP = ("x_lo", "y1", "y0", "core")
QUAD = ("y0", "core")
SUMS = ("x_lo", "y1")
F32 = jnp.float32
BF16 = jnp.bfloat16
SWAP = [(0, 1), (1, 0)]

TOK = 64
TOP = 8
GROUPS = 32
PART = 6
QUADS = 4
ROWS = GROUPS * PART
WIDE = GROUPS * PART * QUADS
BLK = 128
FF = 768
Y = 8
NEXT = 192

PARAMS = pltpu.CompilerParams(vmem_limit_bytes=16 * 1024 * 1024)


def call(kernel, out_shape, operands, flops=0, moved=0):
    vmem = pl.BlockSpec(memory_space=pltpu.VMEM)
    smem = pl.BlockSpec(memory_space=pltpu.SMEM)
    return pl.pallas_call(
        kernel,
        out_shape=out_shape,
        in_specs=[smem if o.dtype == jnp.int32 and o.size == 1 else vmem for o in operands],
        out_specs=jax.tree.map(lambda _: vmem, out_shape, is_leaf=lambda o: hasattr(o, "shape")),
        compiler_params=PARAMS,
        cost_estimate=pl.CostEstimate(flops=flops, bytes_accessed=moved, transcendentals=0),
    )(*operands)


def row_fields(shape, dim):
    r = lax.broadcasted_iota(jnp.int32, shape, dim)
    pair = (r * 2731) >> 16
    rest = r - pair * (QUADS * PART)
    member = (rest * 43) >> 8
    return pair, member, rest - member * PART


def three(value):
    hi = value.astype(BF16)
    left = value - hi.astype(F32)
    mid = left.astype(BF16)
    return hi, mid, (left - mid.astype(F32)).astype(BF16)


def dot(a, b, dims):
    return lax.dot_general(a, b, (dims, ((), ())), preferred_element_type=F32)


def join_kernel(a_ref, b_ref, out_ref):
    out_ref[:, :BLK] = a_ref[...]
    out_ref[:, BLK:] = b_ref[...]


def table_kernel(q_ref, routes_ref, probs_ref, mask_ref, prob_ref, mask_again, prob_again):
    q = q_ref[0]
    shape = (TOK, WIDE)
    pair, member, slot = row_fields(shape, 1)
    chosen = jnp.zeros(shape, F32)
    weight = jnp.zeros(shape, F32)
    for k in range(TOP):
        hit = routes_ref[:, k : k + 1] == pair
        chosen = jnp.where(hit, 1.0, chosen)
        weight = jnp.where(hit, probs_ref[:, k : k + 1], weight)
    row = lax.broadcasted_iota(jnp.int32, (TOK, TOK), 0)
    col = lax.broadcasted_iota(jnp.int32, (TOK, TOK), 1)
    before = jnp.where(col < row, 1.0, 0.0).astype(BF16)
    position = dot(before, chosen.astype(BF16), ((1,), (0,)))
    here = (chosen > 0.5) & (position == (q * PART + slot).astype(F32))
    mask = jnp.where(here, 1.0, 0.0)
    prob = jnp.where(here, weight, 0.0)
    mask_ref[...] = mask.astype(BF16)
    prob_ref[...] = prob
    mask_again[...] = mask.astype(BF16)
    prob_again[...] = prob


def dispatch_kernel(mask_ref, prob_ref, near_ref, far_ref, pay_ref):
    shape = (TOK, WIDE)
    _, member, _ = row_fields(shape, 1)
    mask = mask_ref[...].astype(F32)
    prob = prob_ref[...]
    masks = [jnp.where(member == d, mask, 0.0).astype(BF16) for d in range(QUADS)]
    parts = three(prob)
    x = jnp.zeros((WIDE, BLK), F32)
    dy = jnp.zeros((WIDE, BLK), F32)
    zero = jnp.zeros(shape, BF16)
    for d in range(QUADS):
        source = near_ref if d < 2 else far_ref
        lo = (d % 2) * TOK
        x_tok = source[lo : lo + TOK, :BLK]
        dy_tok = source[lo : lo + TOK, BLK:]
        x = x + dot(masks[d], x_tok, ((0,), (0,)))
        for part in parts:
            dy = dy + dot(jnp.where(member == d, part, zero), dy_tok, ((0,), (0,)))
    pay_ref[:, :BLK] = x.astype(BF16)
    pay_ref[:, BLK:] = dy.astype(BF16)


def place(d):
    i = lax.broadcasted_iota(jnp.int32, (ROWS, WIDE), 0)
    r = lax.broadcasted_iota(jnp.int32, (ROWS, WIDE), 1)
    group = (i * 10923) >> 16
    want = group * (QUADS * PART) + d * PART + (i - group * PART)
    return jnp.where(r == want, 1.0, 0.0).astype(BF16)


def partial_kernel(pay_ref, w0, w1, w2, w3, sums_ref, x_ref, dy_ref):
    got = pay_ref[...]
    for d in range(QUADS):
        moved = dot(place(d), got, ((1,), (0,))).astype(BF16)
        x_ref[:, d * BLK : (d + 1) * BLK] = moved[:, :BLK]
        dy_ref[:, d * BLK : (d + 1) * BLK] = moved[:, BLK:]
    for k in range(3):
        rows_ref = dy_ref if k == 2 else x_ref
        total = jnp.zeros((ROWS, FF), F32)
        for d, w in enumerate((w0, w1, w2, w3)):
            total = total + dot(rows_ref[:, d * BLK : (d + 1) * BLK], w[k], ((1,), (0,)))
        sums_ref[:, k * FF : (k + 1) * FF] = total.astype(BF16)


def act_kernel(in_ref, out_ref):
    rows = ROWS // Y
    for lo in range(0, FF, 256):
        vals = []
        for k in range(3):
            block = in_ref[:, k * FF + lo : k * FF + lo + 256].astype(F32)
            total = block[:rows]
            for y in range(1, Y):
                total = total + block[y * rows : (y + 1) * rows]
            vals.append(total)
        gate, up, back = vals
        s = jax.nn.sigmoid(gate)
        out_ref[:, lo : lo + 256] = (gate * s * up).astype(BF16)
        out_ref[:, FF + lo : FF + lo + 256] = (
            back * up * s * (1.0 + gate * (1.0 - s))
        ).astype(BF16)
        out_ref[:, 2 * FF + lo : 2 * FF + lo + 256] = (back * gate * s).astype(BF16)


def back_kernel(h_ref, w0, w1, w2, w3, pay_ref):
    act = h_ref[:, :FF]
    grad_g = h_ref[:, FF : 2 * FF]
    grad_u = h_ref[:, 2 * FF :]
    total = jnp.zeros((WIDE, 2 * BLK), F32)
    for d, w in enumerate((w0, w1, w2, w3)):
        y = dot(act, w[2], ((1,), (1,)))
        dx = dot(grad_g, w[0], ((1,), (1,))) + dot(grad_u, w[1], ((1,), (1,)))
        both = jnp.concatenate([y.astype(BF16), dx.astype(BF16)], axis=1)
        total = total + dot(place(d), both, ((0,), (0,)))
    pay_ref[...] = total.astype(BF16)


def grad_kernel(h_ref, x_ref, dy_ref, keep_ref, send_ref):
    for d in range(QUADS):
        for k in range(3):
            rows_ref = dy_ref if k == 2 else x_ref
            h_at = (FF, 2 * FF, 0)[k]
            part = dot(
                rows_ref[:, d * BLK : (d + 1) * BLK], h_ref[:, h_at : h_at + FF], ((0,), (0,))
            )
            if d % 2:
                send_ref[d // 2, k] = part.astype(BF16)
            else:
                keep_ref[d // 2, k] = part


def add_near_kernel(keep_ref, near_ref, kept_ref, passed_ref):
    for k in range(3):
        kept_ref[k] = keep_ref[0, k] + near_ref[0, k].astype(F32)
        passed_ref[k] = (keep_ref[1, k] + near_ref[1, k].astype(F32)).astype(BF16)


def combine_kernel(q_ref, pay_ref, mask_ref, prob_ref, out_ref):
    q = q_ref[0]
    shape = (TOK, WIDE)
    _, member, _ = row_fields(shape, 1)
    y = pay_ref[:, :BLK]
    dx = pay_ref[:, BLK:]
    mask = mask_ref[...].astype(F32)
    prob = prob_ref[...]
    for d in range(QUADS):
        at = member == d
        mixed = jnp.zeros((TOK, BLK), F32)
        for part in three(jnp.where(at, prob, 0.0)):
            mixed = mixed + dot(part, y, ((1,), (0,)))
        grad = dot(jnp.where(at, mask, 0.0).astype(BF16), dx, ((1,), (0,)))
        out_ref[q ^ d] = jnp.concatenate([mixed, grad], axis=1).astype(BF16)


def stack_kernel(a_ref, b_ref, c_ref, out_ref):
    for k, ref in enumerate((a_ref, b_ref, c_ref)):
        out_ref[k * NEXT : (k + 1) * NEXT] = ref[...]


def select_kernel(moving_ref, partner_ref, state_ref, a_ref, b_ref, c_ref):
    moving = moving_ref[0] != 0
    for k, ref in enumerate((a_ref, b_ref, c_ref)):
        rows = slice(k * NEXT, (k + 1) * NEXT)
        ref[...] = jnp.where(moving, partner_ref[rows], state_ref[rows])


def shape_of(*dims, dtype=BF16):
    return jax.ShapeDtypeStruct(dims, dtype)


def far_shape(*dims, dtype=BF16):
    return pltpu.HBM(dims, dtype)


def shards(
    tokens,
    grad_out,
    routes,
    gate_probs,
    w_gate,
    w_up,
    w_down,
    dest,
    next_master,
    next_first,
    next_second,
):
    quad = (lax.axis_index("y0") * 2 + lax.axis_index("core")).astype(jnp.int32).reshape(1)

    with jax.named_scope("tokens_to_quad"):
        mine = call(join_kernel, shape_of(TOK, 2 * BLK), (tokens, grad_out), moved=65536)
        near = jnp.concatenate([mine, lax.ppermute(mine, "core", SWAP)], axis=0)
        far = lax.ppermute(near, "y0", SWAP)

    with jax.named_scope("weights_to_quad"):
        w0 = jnp.stack([w_gate[0], w_up[0], w_down[0].T])
        w2 = lax.ppermute(w0, "y0", SWAP)
        w1 = lax.ppermute(w0, "core", SWAP)
        w3 = lax.ppermute(w2, "core", SWAP)

    with jax.named_scope("dispatch"):
        mask, prob, mask_again, prob_again = call(
            table_kernel,
            (
                shape_of(TOK, WIDE),
                shape_of(TOK, WIDE, dtype=F32),
                far_shape(TOK, WIDE),
                far_shape(TOK, WIDE, dtype=F32),
            ),
            (quad, routes, gate_probs),
            flops=2 * TOK * TOK * WIDE,
            moved=300000,
        )
        pay = call(
            dispatch_kernel,
            shape_of(WIDE, 2 * BLK),
            (mask, prob, near, far),
            flops=2 * 16 * TOK * WIDE * BLK,
            moved=800000,
        )
        got = lax.all_to_all(pay, EXPERT, split_axis=0, concat_axis=0, tiled=True)

    with jax.named_scope("relocate"):
        mine_next = [v.reshape(NEXT, BLK) for v in (next_master, next_first, next_second)]
        state = call(stack_kernel, shape_of(3 * NEXT, BLK, dtype=F32), mine_next, moved=600000)

    with jax.named_scope("partial_sums"):
        sums, x_rows, dy_rows = call(
            partial_kernel,
            (far_shape(ROWS, 3 * FF), far_shape(ROWS, 4 * BLK), far_shape(ROWS, 4 * BLK)),
            (got, w0, w1, w2, w3),
            flops=2 * 3 * ROWS * FF * 4 * BLK,
            moved=4000000,
        )
        sums, state = lax.optimization_barrier((sums, state))
        parts = lax.all_to_all(sums, SUMS, split_axis=0, concat_axis=0, tiled=True)
        partner = lax.ppermute(state, "x_hi", SWAP)
        parts, partner = lax.optimization_barrier((parts, partner))

    with jax.named_scope("activation"):
        hidden = call(
            act_kernel, shape_of(ROWS // Y, 3 * FF), (parts,), flops=4000000, moved=1000000
        )
        whole = lax.all_gather(hidden, SUMS, axis=0, tiled=True)

    with jax.named_scope("slot_outputs"):
        back = call(
            back_kernel,
            far_shape(WIDE, 2 * BLK),
            (whole, w0, w1, w2, w3),
            flops=2 * 3 * ROWS * FF * 4 * BLK,
            moved=4000000,
        )
        back, whole = lax.optimization_barrier((back, whole))
        returned = lax.all_to_all(back, EXPERT, split_axis=0, concat_axis=0, tiled=True)

    with jax.named_scope("weight_grads"):
        keep, send = call(
            grad_kernel,
            (shape_of(2, 3, BLK, FF, dtype=F32), shape_of(2, 3, BLK, FF)),
            (whole, x_rows, dy_rows),
            flops=40 * 3 * ROWS * FF * 4 * BLK,
            moved=100000000,
        )
        near_part = lax.ppermute(send, "core", SWAP)
        kept, passed = call(
            add_near_kernel,
            (shape_of(3, BLK, FF, dtype=F32), shape_of(3, BLK, FF)),
            (keep, near_part),
        )
        other = lax.ppermute(passed, "y0", SWAP)
        grads = (kept + other.astype(F32)).astype(BF16)

    with jax.named_scope("combine"):
        mixes = call(
            combine_kernel,
            shape_of(QUADS, TOK, 2 * BLK),
            (quad, returned, mask_again, prob_again),
            flops=2 * 16 * TOK * WIDE * BLK,
            moved=800000,
        )
        mixes = lax.all_to_all(mixes, QUAD, split_axis=0, concat_axis=0, tiled=True)
        mixes = jnp.sum(mixes.astype(F32), axis=0).astype(BF16)

    with jax.named_scope("relocate"):
        moving = (dest != lax.axis_index(EXPERT).astype(jnp.int32)).astype(jnp.int32)
        moved = call(
            select_kernel,
            [shape_of(NEXT, BLK, dtype=F32)] * 3,
            (moving, partner, state),
            moved=1200000,
        )
        moved = [v.reshape(next_master.shape) for v in moved]

    return (
        mixes[:, :BLK],
        mixes[:, BLK:],
        grads[0][None],
        grads[1][None],
        grads[2].T[None],
        moved[0],
        moved[1],
        moved[2],
    )


def solution(mesh):
    fine = Mesh(
        mesh.devices.reshape(2, 4, 2, 2, 2, 16), ("x_lo", "y1", "y0", "core", "x_hi", "z")
    )
    return jax.shard_map(
        shards,
        mesh=fine,
        in_specs=(
            P(EXPERT, DP),
            P(EXPERT, DP),
            P(EXPERT, None),
            P(EXPERT, None),
            P(EXPERT, DP, None),
            P(EXPERT, DP, None),
            P(EXPERT, None, DP),
            P(EXPERT),
            P(EXPERT, DP, None),
            P(EXPERT, DP, None),
            P(EXPERT, DP, None),
        ),
        out_specs=(
            P(EXPERT, DP),
            P(EXPERT, DP),
            P(EXPERT, DP, None),
            P(EXPERT, DP, None),
            P(EXPERT, None, DP),
            P(EXPERT, DP, None),
            P(EXPERT, DP, None),
            P(EXPERT, DP, None),
        ),
        check_vma=False,
    )
```

```python
import functools

import jax
import jax.numpy as jnp
from jax import lax
from jax.experimental import pallas as pl
from jax.experimental.pallas import tpu as pltpu
from jax.sharding import Mesh
from jax.sharding import PartitionSpec as P

EXPERT = ("x_hi", "z")
DP = ("x_lo", "y1", "y0", "core")
QUAD = ("y0", "core")
SUMS = ("x_lo", "y1")
F32 = jnp.float32
BF16 = jnp.bfloat16
SWAP = [(0, 1), (1, 0)]

TOK = 64
TOP = 8
GROUPS = 32
PART = 6
QUADS = 4
ROWS = GROUPS * PART
WIDE = GROUPS * PART * QUADS
BLK = 128
FF = 768
Y = 8
NEXT = 192

PARAMS = pltpu.CompilerParams(vmem_limit_bytes=16 * 1024 * 1024)


def call(kernel, out_shape, operands, flops=0, moved=0):
    vmem = pl.BlockSpec(memory_space=pltpu.VMEM)
    smem = pl.BlockSpec(memory_space=pltpu.SMEM)
    return pl.pallas_call(
        kernel,
        out_shape=out_shape,
        in_specs=[smem if o.dtype == jnp.int32 and o.size == 1 else vmem for o in operands],
        out_specs=jax.tree.map(lambda _: vmem, out_shape, is_leaf=lambda o: hasattr(o, "shape")),
        compiler_params=PARAMS,
        cost_estimate=pl.CostEstimate(flops=flops, bytes_accessed=moved, transcendentals=0),
    )(*operands)


def row_fields(shape, dim):
    r = lax.broadcasted_iota(jnp.int32, shape, dim)
    pair = (r * 2731) >> 16
    rest = r - pair * (QUADS * PART)
    member = (rest * 43) >> 8
    return pair, member, rest - member * PART


def three(value):
    hi = value.astype(BF16)
    left = value - hi.astype(F32)
    mid = left.astype(BF16)
    return hi, mid, (left - mid.astype(F32)).astype(BF16)


def dot(a, b, dims):
    return lax.dot_general(a, b, (dims, ((), ())), preferred_element_type=F32)


def join_kernel(a_ref, b_ref, out_ref, sem_a, sem_b):
    copies = [
        pltpu.make_async_copy(a_ref, out_ref.at[:, :BLK], sem_a),
        pltpu.make_async_copy(b_ref, out_ref.at[:, BLK:], sem_b),
    ]
    for copy in copies:
        copy.start()
    for copy in copies:
        copy.wait()


def join(a, b):
    hbm = pl.BlockSpec(memory_space=pltpu.HBM)
    return pl.pallas_call(
        join_kernel,
        out_shape=shape_of(TOK, 2 * BLK),
        in_specs=[hbm, hbm],
        out_specs=pl.BlockSpec(memory_space=pltpu.VMEM),
        scratch_shapes=[pltpu.SemaphoreType.DMA, pltpu.SemaphoreType.DMA],
        compiler_params=PARAMS,
        cost_estimate=pl.CostEstimate(flops=0, bytes_accessed=65536, transcendentals=0),
    )(*[pltpu.with_memory_space_constraint(v, pltpu.HBM) for v in (a, b)])


def table_kernel(q_ref, routes_ref, probs_ref, mask_ref, prob_ref, mask_again, prob_again):
    q = q_ref[0]
    shape = (TOK, WIDE)
    pair, member, slot = row_fields(shape, 1)
    chosen = jnp.zeros(shape, F32)
    weight = jnp.zeros(shape, F32)
    expert = pair.astype(F32)
    row = lax.broadcasted_iota(jnp.int32, (TOK, TOK), 0)
    col = lax.broadcasted_iota(jnp.int32, (TOK, TOK), 1)
    unit = jnp.where(col == row, 1.0, 0.0).astype(BF16)
    routes = dot(unit, routes_ref[...].astype(F32).astype(BF16), ((1,), (1,)))
    hi, mid, low = [dot(unit, part, ((1,), (1,))) for part in three(probs_ref[...])]
    probs = (hi + mid) + low
    for k in range(TOP):
        hit = routes[:, k : k + 1] == expert
        chosen = jnp.where(hit, 1.0, chosen)
        weight = jnp.where(hit, probs[:, k : k + 1], weight)
    before = jnp.where(col < row, 1.0, 0.0).astype(BF16)
    position = dot(before, chosen.astype(BF16), ((1,), (0,)))
    here = (chosen > 0.5) & (position == (q * PART + slot).astype(F32))
    mask = jnp.where(here, 1.0, 0.0)
    prob = jnp.where(here, weight, 0.0)
    mask_ref[...] = mask.astype(BF16)
    prob_ref[...] = prob
    mask_again[...] = mask.astype(BF16)
    prob_again[...] = prob


def dispatch_kernel(mask_ref, prob_ref, near_ref, far_ref, pay_ref):
    shape = (TOK, WIDE)
    _, member, _ = row_fields(shape, 1)
    mask = mask_ref[...].astype(F32)
    prob = prob_ref[...]
    masks = [jnp.where(member == d, mask, 0.0).astype(BF16) for d in range(QUADS)]
    parts = three(prob)
    x = jnp.zeros((WIDE, BLK), F32)
    dy = jnp.zeros((WIDE, BLK), F32)
    zero = jnp.zeros(shape, BF16)
    for d in range(QUADS):
        source = near_ref if d < 2 else far_ref
        lo = (d % 2) * TOK
        x_tok = source[lo : lo + TOK, :BLK]
        dy_tok = source[lo : lo + TOK, BLK:]
        x = x + dot(masks[d], x_tok, ((0,), (0,)))
        for part in parts:
            dy = dy + dot(jnp.where(member == d, part, zero), dy_tok, ((0,), (0,)))
    pay_ref[:, :BLK] = x.astype(BF16)
    pay_ref[:, BLK:] = dy.astype(BF16)


def place(d):
    i = lax.broadcasted_iota(jnp.int32, (ROWS, WIDE), 0)
    r = lax.broadcasted_iota(jnp.int32, (ROWS, WIDE), 1)
    group = (i * 10923) >> 16
    want = group * (QUADS * PART) + d * PART + (i - group * PART)
    return jnp.where(r == want, 1.0, 0.0).astype(BF16)


def partial_kernel(pay_ref, w0, w1, w2, w3, sums_ref, x_ref, dy_ref):
    got = pay_ref[...]
    for d in range(QUADS):
        moved = dot(place(d), got, ((1,), (0,))).astype(BF16)
        x_ref[:, d * BLK : (d + 1) * BLK] = moved[:, :BLK]
        dy_ref[:, d * BLK : (d + 1) * BLK] = moved[:, BLK:]
    for k in range(3):
        rows_ref = dy_ref if k == 2 else x_ref
        total = jnp.zeros((ROWS, FF), F32)
        for d, w in enumerate((w0, w1, w2, w3)):
            total = total + dot(rows_ref[:, d * BLK : (d + 1) * BLK], w[k], ((1,), (0,)))
        sums_ref[:, k * FF : (k + 1) * FF] = total.astype(BF16)


def act_kernel(in_ref, out_ref):
    rows = ROWS // Y
    for lo in range(0, FF, 256):
        vals = []
        for k in range(3):
            block = in_ref[:, k * FF + lo : k * FF + lo + 256].astype(F32)
            total = block[:rows]
            for y in range(1, Y):
                total = total + block[y * rows : (y + 1) * rows]
            vals.append(total)
        gate, up, back = vals
        s = jax.nn.sigmoid(gate)
        act = gate * s * up
        grad_g = back * up * s * (1.0 + gate * (1.0 - s))
        grad_u = back * gate * s
        for k, value in enumerate((act, grad_g, grad_u)):
            at = slice(k * FF + lo, k * FF + lo + 256)
            out_ref[:, at] = jnp.concatenate([value] * Y, axis=0).astype(BF16)


def place_back(d):
    pair, member, slot = row_fields((WIDE, ROWS), 0)
    col = lax.broadcasted_iota(jnp.int32, (WIDE, ROWS), 1)
    return jnp.where((member == d) & (col == pair * PART + slot), 1.0, 0.0).astype(BF16)


def back_kernel(h_ref, w0, w1, w2, w3, pay_ref):
    act = h_ref[:, :FF]
    grad_g = h_ref[:, FF : 2 * FF]
    grad_u = h_ref[:, 2 * FF :]
    total = jnp.zeros((WIDE, 2 * BLK), F32)
    for d, w in enumerate((w0, w1, w2, w3)):
        y = dot(act, w[2], ((1,), (1,)))
        dx = dot(grad_g, w[0], ((1,), (1,))) + dot(grad_u, w[1], ((1,), (1,)))
        both = jnp.concatenate([y.astype(BF16), dx.astype(BF16)], axis=1)
        total = total + dot(place_back(d), both, ((1,), (0,)))
    pay_ref[...] = total.astype(BF16)


def grad_kernel(h_ref, x_ref, dy_ref, keep_ref, send_ref):
    for d in range(QUADS):
        for k in range(3):
            rows_ref = dy_ref if k == 2 else x_ref
            h_at = (FF, 2 * FF, 0)[k]
            part = dot(
                rows_ref[:, d * BLK : (d + 1) * BLK], h_ref[:, h_at : h_at + FF], ((0,), (0,))
            )
            if d % 2:
                send_ref[d // 2, k] = part.astype(BF16)
            else:
                keep_ref[d // 2, k] = part


def add_near_kernel(keep_ref, near_ref, kept_ref, passed_ref):
    for k in range(3):
        kept_ref[k] = keep_ref[0, k] + near_ref[0, k].astype(F32)
        passed_ref[k] = (keep_ref[1, k] + near_ref[1, k].astype(F32)).astype(BF16)


def add_far_kernel(kept_ref, other_ref, gate_ref, up_ref, down_ref):
    gate_ref[...] = (kept_ref[0] + other_ref[0].astype(F32)).astype(BF16)
    up_ref[...] = (kept_ref[1] + other_ref[1].astype(F32)).astype(BF16)
    down_ref[...] = (kept_ref[2] + other_ref[2].astype(F32)).T.astype(BF16)


def mix_kernel(in_ref, mixed_ref, grad_ref):
    total = in_ref[0].astype(F32)
    for d in range(1, QUADS):
        total = total + in_ref[d].astype(F32)
    mixed_ref[...] = total[:, :BLK].astype(BF16)
    grad_ref[...] = total[:, BLK:].astype(BF16)


def combine_kernel(q_ref, pay_ref, mask_ref, prob_ref, out_ref):
    q = q_ref[0]
    shape = (TOK, WIDE)
    _, member, _ = row_fields(shape, 1)
    y = pay_ref[:, :BLK]
    dx = pay_ref[:, BLK:]
    mask = mask_ref[...].astype(F32)
    prob = prob_ref[...]
    for d in range(QUADS):
        at = member == d
        mixed = jnp.zeros((TOK, BLK), F32)
        for part in three(jnp.where(at, prob, 0.0)):
            mixed = mixed + dot(part, y, ((1,), (0,)))
        grad = dot(jnp.where(at, mask, 0.0).astype(BF16), dx, ((1,), (0,)))
        out_ref[q ^ d] = jnp.concatenate([mixed, grad], axis=1).astype(BF16)


def stack_kernel(a_ref, b_ref, c_ref, out_ref):
    for k, ref in enumerate((a_ref, b_ref, c_ref)):
        out_ref[k * NEXT : (k + 1) * NEXT] = ref[...]


def select_kernel(moving_ref, partner_ref, state_ref, a_ref, b_ref, c_ref):
    moving = moving_ref[0] != 0
    for k, ref in enumerate((a_ref, b_ref, c_ref)):
        rows = slice(k * NEXT, (k + 1) * NEXT)
        ref[...] = jnp.where(moving, partner_ref[rows], state_ref[rows])


def shape_of(*dims, dtype=BF16):
    return jax.ShapeDtypeStruct(dims, dtype)


def far_shape(*dims, dtype=BF16):
    return pltpu.HBM(dims, dtype)


def shards(
    tokens,
    grad_out,
    routes,
    gate_probs,
    w_gate,
    w_up,
    w_down,
    dest,
    next_master,
    next_first,
    next_second,
):
    quad = (lax.axis_index("y0") * 2 + lax.axis_index("core")).astype(jnp.int32).reshape(1)

    with jax.named_scope("tokens_to_quad"):
        mine = join(tokens, grad_out)
        near = jnp.concatenate([mine, lax.ppermute(mine, "core", SWAP)], axis=0)
        far = lax.ppermute(near, "y0", SWAP)

    with jax.named_scope("weights_to_quad"):
        w0 = jnp.stack([w_gate[0], w_up[0], w_down[0].T])
        w2 = lax.ppermute(w0, "y0", SWAP)
        w1 = lax.ppermute(w0, "core", SWAP)
        w3 = lax.ppermute(w2, "core", SWAP)

    with jax.named_scope("dispatch"):
        mask, prob, mask_again, prob_again = call(
            table_kernel,
            (
                shape_of(TOK, WIDE),
                shape_of(TOK, WIDE, dtype=F32),
                far_shape(TOK, WIDE),
                far_shape(TOK, WIDE, dtype=F32),
            ),
            (quad, routes.T, gate_probs.T),
            flops=2 * TOK * TOK * WIDE,
            moved=300000,
        )
        pay = call(
            dispatch_kernel,
            shape_of(WIDE, 2 * BLK),
            (mask, prob, near, far),
            flops=2 * 16 * TOK * WIDE * BLK,
            moved=800000,
        )
        got = lax.all_to_all(pay, EXPERT, split_axis=0, concat_axis=0, tiled=True)

    with jax.named_scope("relocate"):
        mine_next = [v.reshape(NEXT, BLK) for v in (next_master, next_first, next_second)]
        state = call(stack_kernel, shape_of(3 * NEXT, BLK, dtype=F32), mine_next, moved=600000)

    with jax.named_scope("partial_sums"):
        sums, x_rows, dy_rows = call(
            partial_kernel,
            (far_shape(ROWS, 3 * FF), far_shape(ROWS, 4 * BLK), far_shape(ROWS, 4 * BLK)),
            (got, w0, w1, w2, w3),
            flops=2 * 3 * ROWS * FF * 4 * BLK,
            moved=4000000,
        )
        sums, state = lax.optimization_barrier((sums, state))
        parts = lax.all_to_all(sums, SUMS, split_axis=0, concat_axis=0, tiled=True)
        partner = lax.ppermute(state, "x_hi", SWAP)
        parts, partner = lax.optimization_barrier((parts, partner))

    with jax.named_scope("activation"):
        hidden = call(
            act_kernel, far_shape(ROWS, 3 * FF), (parts,), flops=4000000, moved=1000000
        )
        whole = lax.all_to_all(hidden, SUMS, split_axis=0, concat_axis=0, tiled=True)

    with jax.named_scope("slot_outputs"):
        back = call(
            back_kernel,
            far_shape(WIDE, 2 * BLK),
            (whole, w0, w1, w2, w3),
            flops=2 * 3 * ROWS * FF * 4 * BLK,
            moved=4000000,
        )
        back, whole = lax.optimization_barrier((back, whole))
        returned = lax.all_to_all(back, EXPERT, split_axis=0, concat_axis=0, tiled=True)

    with jax.named_scope("weight_grads"):
        keep, send = call(
            grad_kernel,
            (shape_of(2, 3, BLK, FF, dtype=F32), shape_of(2, 3, BLK, FF)),
            (whole, x_rows, dy_rows),
            flops=40 * 3 * ROWS * FF * 4 * BLK,
            moved=100000000,
        )
        near_part = lax.ppermute(send, "core", SWAP)
        kept, passed = call(
            add_near_kernel,
            (far_shape(3, BLK, FF, dtype=F32), shape_of(3, BLK, FF)),
            (keep, near_part),
        )
        other = lax.ppermute(passed, "y0", SWAP)
        grads = call(
            add_far_kernel,
            (far_shape(BLK, FF), far_shape(BLK, FF), far_shape(FF, BLK)),
            (kept, other),
            flops=300000,
            moved=3000000,
        )

    with jax.named_scope("combine"):
        mixes = call(
            combine_kernel,
            shape_of(QUADS, TOK, 2 * BLK),
            (quad, returned, mask_again, prob_again),
            flops=2 * 16 * TOK * WIDE * BLK,
            moved=800000,
        )
        mixes = lax.all_to_all(mixes, QUAD, split_axis=0, concat_axis=0, tiled=True)
        mixed, token_grad = call(
            mix_kernel, (far_shape(TOK, BLK), far_shape(TOK, BLK)), (mixes,), moved=200000
        )

    with jax.named_scope("relocate"):
        moving = (dest != lax.axis_index(EXPERT).astype(jnp.int32)).astype(jnp.int32)
        moved = call(
            select_kernel,
            [shape_of(NEXT, BLK, dtype=F32)] * 3,
            (moving, partner, state),
            moved=1200000,
        )
        moved = [v.reshape(next_master.shape) for v in moved]

    return (
        mixed,
        token_grad,
        grads[0][None],
        grads[1][None],
        grads[2][None],
        moved[0],
        moved[1],
        moved[2],
    )


def solution(mesh):
    fine = Mesh(
        mesh.devices.reshape(2, 4, 2, 2, 2, 16), ("x_lo", "y1", "y0", "core", "x_hi", "z")
    )
    return jax.shard_map(
        shards,
        mesh=fine,
        in_specs=(
            P(EXPERT, DP),
            P(EXPERT, DP),
            P(EXPERT, None),
            P(EXPERT, None),
            P(EXPERT, DP, None),
            P(EXPERT, DP, None),
            P(EXPERT, None, DP),
            P(EXPERT),
            P(EXPERT, DP, None),
            P(EXPERT, DP, None),
            P(EXPERT, DP, None),
        ),
        out_specs=(
            P(EXPERT, DP),
            P(EXPERT, DP),
            P(EXPERT, DP, None),
            P(EXPERT, DP, None),
            P(EXPERT, None, DP),
            P(EXPERT, DP, None),
            P(EXPERT, DP, None),
            P(EXPERT, DP, None),
        ),
        check_vma=False,
    )
```

```python
import functools

import jax
import jax.numpy as jnp
from jax import lax
from jax.experimental import pallas as pl
from jax.experimental.pallas import tpu as pltpu
from jax.sharding import Mesh
from jax.sharding import PartitionSpec as P

EXPERT = ("x_hi", "z")
DP = ("x_lo", "y1", "y0", "core")
QUAD = ("y0", "core")
SUMS = ("x_lo", "y1")
F32 = jnp.float32
BF16 = jnp.bfloat16
SWAP = [(0, 1), (1, 0)]

TOK = 64
TOP = 8
GROUPS = 32
PART = 6
QUADS = 4
ROWS = GROUPS * PART
WIDE = GROUPS * PART * QUADS
BLK = 128
FF = 768
Y = 8
NEXT = 192

PARAMS = pltpu.CompilerParams(vmem_limit_bytes=16 * 1024 * 1024)


def far(value):
    return pltpu.with_memory_space_constraint(value, pltpu.HBM)


def call(kernel, out_shape, operands, flops=0, moved=0):
    vmem = pl.BlockSpec(memory_space=pltpu.VMEM)
    smem = pl.BlockSpec(memory_space=pltpu.SMEM)
    return pl.pallas_call(
        kernel,
        out_shape=out_shape,
        in_specs=[smem if o.dtype == jnp.int32 and o.size == 1 else vmem for o in operands],
        out_specs=jax.tree.map(lambda _: vmem, out_shape, is_leaf=lambda o: hasattr(o, "shape")),
        compiler_params=PARAMS,
        cost_estimate=pl.CostEstimate(flops=flops, bytes_accessed=moved, transcendentals=0),
    )(*operands)


def row_fields(shape, dim):
    r = lax.broadcasted_iota(jnp.int32, shape, dim)
    pair = (r * 2731) >> 16
    rest = r - pair * (QUADS * PART)
    member = (rest * 43) >> 8
    return pair, member, rest - member * PART


def three(value):
    hi = value.astype(BF16)
    left = value - hi.astype(F32)
    mid = left.astype(BF16)
    return hi, mid, (left - mid.astype(F32)).astype(BF16)


def dot(a, b, dims):
    return lax.dot_general(a, b, (dims, ((), ())), preferred_element_type=F32)


def join_kernel(a_ref, b_ref, out_ref, sem_a, sem_b):
    copies = [
        pltpu.make_async_copy(a_ref, out_ref.at[:, :BLK], sem_a),
        pltpu.make_async_copy(b_ref, out_ref.at[:, BLK:], sem_b),
    ]
    for copy in copies:
        copy.start()
    for copy in copies:
        copy.wait()


def join(a, b):
    hbm = pl.BlockSpec(memory_space=pltpu.HBM)
    return pl.pallas_call(
        join_kernel,
        out_shape=shape_of(TOK, 2 * BLK),
        in_specs=[hbm, hbm],
        out_specs=pl.BlockSpec(memory_space=pltpu.VMEM),
        scratch_shapes=[pltpu.SemaphoreType.DMA, pltpu.SemaphoreType.DMA],
        compiler_params=PARAMS,
        cost_estimate=pl.CostEstimate(flops=0, bytes_accessed=65536, transcendentals=0),
    )(far(a), far(b))


def table_kernel(q_ref, routes_ref, probs_ref, prob_ref, prob_again):
    q = q_ref[0]
    shape = (TOK, WIDE)
    pair, member, slot = row_fields(shape, 1)
    chosen = jnp.zeros(shape, F32)
    weight = jnp.zeros(shape, F32)
    expert = pair.astype(F32)
    row = lax.broadcasted_iota(jnp.int32, (TOK, TOK), 0)
    col = lax.broadcasted_iota(jnp.int32, (TOK, TOK), 1)
    unit = jnp.where(col == row, 1.0, 0.0).astype(BF16)
    routes = dot(unit, routes_ref[...].astype(F32).astype(BF16), ((1,), (1,)))
    hi, mid, low = [dot(unit, part, ((1,), (1,))) for part in three(probs_ref[...])]
    probs = (hi + mid) + low
    for k in range(TOP):
        hit = routes[:, k : k + 1] == expert
        chosen = jnp.where(hit, 1.0, chosen)
        weight = jnp.where(hit, probs[:, k : k + 1], weight)
    before = jnp.where(col < row, 1.0, 0.0).astype(BF16)
    position = dot(before, chosen.astype(BF16), ((1,), (0,)))
    here = (chosen > 0.5) & (position == (q * PART + slot).astype(F32))
    prob = jnp.where(here, weight, 0.0)
    prob_ref[...] = prob
    prob_again[...] = prob


def dispatch_kernel(prob_ref, near_ref, far_ref, pay_ref):
    shape = (TOK, WIDE)
    _, member, _ = row_fields(shape, 1)
    prob = prob_ref[...]
    mask = jnp.where(prob > 0.0, 1.0, 0.0)
    masks = [jnp.where(member == d, mask, 0.0).astype(BF16) for d in range(QUADS)]
    parts = three(prob)
    x = jnp.zeros((WIDE, BLK), F32)
    dy = jnp.zeros((WIDE, BLK), F32)
    zero = jnp.zeros(shape, BF16)
    for d in range(QUADS):
        source = near_ref if d < 2 else far_ref
        lo = (d % 2) * TOK
        x_tok = source[lo : lo + TOK, :BLK]
        dy_tok = source[lo : lo + TOK, BLK:]
        x = x + dot(masks[d], x_tok, ((0,), (0,)))
        for part in parts:
            dy = dy + dot(jnp.where(member == d, part, zero), dy_tok, ((0,), (0,)))
    pay_ref[:, :BLK] = x.astype(BF16)
    pay_ref[:, BLK:] = dy.astype(BF16)


def place(d):
    i = lax.broadcasted_iota(jnp.int32, (ROWS, WIDE), 0)
    r = lax.broadcasted_iota(jnp.int32, (ROWS, WIDE), 1)
    group = (i * 10923) >> 16
    want = group * (QUADS * PART) + d * PART + (i - group * PART)
    return jnp.where(r == want, 1.0, 0.0).astype(BF16)


def partial_kernel(pay_ref, w0, w1, w2, w3, sums_hbm, x_hbm, dy_hbm, sums_ref, rows_ref, sems):
    got = pay_ref[...]
    for d in range(QUADS):
        moved = dot(place(d), got, ((1,), (0,))).astype(BF16)
        rows_ref[0, :, d * BLK : (d + 1) * BLK] = moved[:, :BLK]
        rows_ref[1, :, d * BLK : (d + 1) * BLK] = moved[:, BLK:]
    copies = [
        pltpu.make_async_copy(rows_ref.at[0], x_hbm, sems.at[3]),
        pltpu.make_async_copy(rows_ref.at[1], dy_hbm, sems.at[4]),
    ]
    for k in range(3):
        rows = rows_ref[k // 2]
        low = jnp.concatenate([w0[k], w1[k]], axis=0)
        high = jnp.concatenate([w2[k], w3[k]], axis=0)
        total = dot(rows[:, : 2 * BLK], low, ((1,), (0,))) + dot(
            rows[:, 2 * BLK :], high, ((1,), (0,))
        )
        at = slice(k * FF, (k + 1) * FF)
        sums_ref[:, at] = total.astype(BF16)
        copies.append(pltpu.make_async_copy(sums_ref.at[:, at], sums_hbm.at[:, at], sems.at[k]))
        copies[-1].start()
    copies[0].start()
    copies[1].start()
    for copy in copies:
        copy.wait()


def partial_sums(*operands):
    vmem, hbm = [pl.BlockSpec(memory_space=m) for m in (pltpu.VMEM, pltpu.HBM)]
    return pl.pallas_call(
        partial_kernel,
        out_shape=(far_shape(ROWS, 3 * FF), far_shape(ROWS, 4 * BLK), far_shape(ROWS, 4 * BLK)),
        in_specs=[vmem] * 5,
        out_specs=[hbm] * 3,
        scratch_shapes=[
            pltpu.VMEM((ROWS, 3 * FF), BF16),
            pltpu.VMEM((2, ROWS, 4 * BLK), BF16),
            pltpu.SemaphoreType.DMA((5,)),
        ],
        compiler_params=PARAMS,
        cost_estimate=pl.CostEstimate(
            flops=2 * 3 * ROWS * FF * 4 * BLK, bytes_accessed=4000000, transcendentals=0
        ),
    )(*operands)


def act_kernel(in_ref, out_ref):
    rows = ROWS // Y
    for lo in range(0, FF, 256):
        vals = []
        for k in range(3):
            block = in_ref[:, k * FF + lo : k * FF + lo + 256].astype(F32)
            total = block[:rows]
            for y in range(1, Y):
                total = total + block[y * rows : (y + 1) * rows]
            vals.append(total)
        gate, up, back = vals
        s = jax.nn.sigmoid(gate)
        act = gate * s * up
        grad_g = back * up * s * (1.0 + gate * (1.0 - s))
        grad_u = back * gate * s
        for k, value in enumerate((act, grad_g, grad_u)):
            at = slice(k * FF + lo, k * FF + lo + 256)
            out_ref[:, at] = jnp.concatenate([value] * Y, axis=0).astype(BF16)


def back_kernel(h_ref, w0, w1, w2, w3, pay_ref):
    act = h_ref[:, :FF]
    grad_g = h_ref[:, FF : 2 * FF]
    grad_u = h_ref[:, 2 * FF :]
    pair, member, slot = row_fields((WIDE, ROWS), 0)
    source = member * ROWS + pair * PART + slot
    col = lax.broadcasted_iota(jnp.int32, (WIDE, ROWS), 1)
    total = jnp.zeros((WIDE, 2 * BLK), F32)
    for p, (wa, wb) in enumerate(((w0, w1), (w2, w3))):
        weights = [jnp.concatenate([wa[k], wb[k]], axis=0) for k in range(3)]
        y = dot(act, weights[2], ((1,), (1,))).astype(BF16)
        dx = dot(grad_g, weights[0], ((1,), (1,))) + dot(grad_u, weights[1], ((1,), (1,)))
        dx = dx.astype(BF16)
        for h in range(2):
            both = jnp.concatenate([v[:, h * BLK : (h + 1) * BLK] for v in (y, dx)], axis=1)
            onehot = jnp.where(source == col + (2 * p + h) * ROWS, 1.0, 0.0).astype(BF16)
            total = total + dot(onehot, both, ((1,), (0,)))
    pay_ref[...] = total.astype(BF16)


def grad_kernel(h_ref, x_ref, dy_ref, keep_ref, send_ref):
    for d in range(QUADS):
        for k in range(3):
            rows_ref = dy_ref if k == 2 else x_ref
            h_at = (FF, 2 * FF, 0)[k]
            part = dot(
                rows_ref[:, d * BLK : (d + 1) * BLK], h_ref[:, h_at : h_at + FF], ((0,), (0,))
            )
            if d % 2:
                send_ref[d // 2, k] = part.astype(BF16)
            else:
                keep_ref[d // 2, k] = part


def add_near_kernel(keep_ref, near_ref, kept_ref, passed_ref):
    for k in range(3):
        kept_ref[k] = keep_ref[0, k] + near_ref[0, k].astype(F32)
        passed_ref[k] = (keep_ref[1, k] + near_ref[1, k].astype(F32)).astype(BF16)


def add_far_kernel(kept_ref, other_ref, gate_ref, up_ref, down_ref):
    gate_ref[...] = (kept_ref[0] + other_ref[0].astype(F32)).astype(BF16)
    up_ref[...] = (kept_ref[1] + other_ref[1].astype(F32)).astype(BF16)
    down_ref[...] = (kept_ref[2] + other_ref[2].astype(F32)).T.astype(BF16)


def combine_kernel(q_ref, pay_ref, prob_ref, out_ref):
    q = q_ref[0]
    shape = (TOK, WIDE)
    _, member, _ = row_fields(shape, 1)
    y = pay_ref[:, :BLK]
    dx = pay_ref[:, BLK:]
    prob = prob_ref[...]
    mask = jnp.where(prob > 0.0, 1.0, 0.0)
    for d in range(QUADS):
        at = member == d
        mixed = jnp.zeros((TOK, BLK), F32)
        for part in three(jnp.where(at, prob, 0.0)):
            mixed = mixed + dot(part, y, ((1,), (0,)))
        grad = dot(jnp.where(at, mask, 0.0).astype(BF16), dx, ((1,), (0,)))
        out_ref[q ^ d] = jnp.concatenate([mixed, grad], axis=1).astype(BF16)


def stack_kernel(a_ref, b_ref, c_ref, out_ref):
    for k, ref in enumerate((a_ref, b_ref, c_ref)):
        out_ref[k * NEXT : (k + 1) * NEXT] = ref[...]


def select_kernel(moving_ref, partner_ref, state_ref, a_ref, b_ref, c_ref):
    moving = moving_ref[0] != 0
    for k, ref in enumerate((a_ref, b_ref, c_ref)):
        rows = slice(k * NEXT, (k + 1) * NEXT)
        ref[...] = jnp.where(moving, partner_ref[rows], state_ref[rows])


def shape_of(*dims, dtype=BF16):
    return jax.ShapeDtypeStruct(dims, dtype)


def far_shape(*dims, dtype=BF16):
    return pltpu.HBM(dims, dtype)


def shards(
    tokens,
    grad_out,
    routes,
    gate_probs,
    w_gate,
    w_up,
    w_down,
    dest,
    next_master,
    next_first,
    next_second,
):
    quad = (lax.axis_index("y0") * 2 + lax.axis_index("core")).astype(jnp.int32).reshape(1)

    with jax.named_scope("tokens_to_quad"):
        mine = join(tokens, grad_out)
        near = jnp.concatenate([mine, lax.ppermute(mine, "core", SWAP)], axis=0)
        far_tokens = lax.ppermute(near, "y0", SWAP)

    with jax.named_scope("weights_to_quad"):
        w0 = jnp.stack([w_gate[0], w_up[0], w_down[0].T])
        w2 = lax.ppermute(w0, "y0", SWAP)
        w1 = lax.ppermute(w0, "core", SWAP)
        w3 = lax.ppermute(w2, "core", SWAP)

    with jax.named_scope("dispatch"):
        prob, prob_again = call(
            table_kernel,
            (shape_of(TOK, WIDE, dtype=F32), far_shape(TOK, WIDE, dtype=F32)),
            (quad, far(routes.T), far(gate_probs.T)),
            flops=2 * TOK * TOK * WIDE,
            moved=300000,
        )
        pay = call(
            dispatch_kernel,
            shape_of(WIDE, 2 * BLK),
            (prob, near, far_tokens),
            flops=2 * 16 * TOK * WIDE * BLK,
            moved=800000,
        )
        got = lax.all_to_all(pay, EXPERT, split_axis=0, concat_axis=0, tiled=True)

    with jax.named_scope("relocate"):
        mine_next = [v.reshape(NEXT, BLK) for v in (next_master, next_first, next_second)]
        state = call(stack_kernel, shape_of(3 * NEXT, BLK, dtype=F32), mine_next, moved=600000)

    with jax.named_scope("partial_sums"):
        sums, x_rows, dy_rows = partial_sums(got, w0, w1, w2, w3)
        sums, state = lax.optimization_barrier((sums, state))
        parts = lax.all_to_all(sums, SUMS, split_axis=0, concat_axis=0, tiled=True)
        partner = lax.ppermute(state, "x_hi", SWAP)
        parts, partner = lax.optimization_barrier((parts, partner))

    with jax.named_scope("activation"):
        hidden = call(
            act_kernel, far_shape(ROWS, 3 * FF), (parts,), flops=4000000, moved=1000000
        )
        whole = lax.all_to_all(hidden, SUMS, split_axis=0, concat_axis=0, tiled=True)

    with jax.named_scope("slot_outputs"):
        back = call(
            back_kernel,
            far_shape(WIDE, 2 * BLK),
            (whole, w0, w1, w2, w3),
            flops=2 * 3 * ROWS * FF * 4 * BLK,
            moved=4000000,
        )
        back, whole = lax.optimization_barrier((back, whole))
        returned = lax.all_to_all(back, EXPERT, split_axis=0, concat_axis=0, tiled=True)

    with jax.named_scope("weight_grads"):
        keep, send = call(
            grad_kernel,
            (shape_of(2, 3, BLK, FF, dtype=F32), shape_of(2, 3, BLK, FF)),
            (whole, x_rows, dy_rows),
            flops=40 * 3 * ROWS * FF * 4 * BLK,
            moved=100000000,
        )
        near_part = lax.ppermute(send, "core", SWAP)
        kept, passed = call(
            add_near_kernel,
            (far_shape(3, BLK, FF, dtype=F32), shape_of(3, BLK, FF)),
            (keep, near_part),
        )
        other = lax.ppermute(passed, "y0", SWAP)
        grads = call(
            add_far_kernel,
            (far_shape(BLK, FF), far_shape(BLK, FF), far_shape(FF, BLK)),
            (kept, other),
            flops=300000,
            moved=3000000,
        )

    with jax.named_scope("combine"):
        mixes = call(
            combine_kernel,
            shape_of(QUADS, TOK, 2 * BLK),
            (quad, returned, far(prob_again)),
            flops=2 * 16 * TOK * WIDE * BLK,
            moved=800000,
        )
        mixes = lax.all_to_all(mixes, QUAD, split_axis=0, concat_axis=0, tiled=True)
        mixes = jnp.sum(mixes.astype(F32), axis=0).astype(BF16)
        mixed, token_grad = mixes[:, :BLK], mixes[:, BLK:]

    with jax.named_scope("relocate"):
        moving = (dest != lax.axis_index(EXPERT).astype(jnp.int32)).astype(jnp.int32)
        moved = call(
            select_kernel,
            [shape_of(NEXT, BLK, dtype=F32)] * 3,
            (moving, partner, state),
            moved=1200000,
        )
        moved = [v.reshape(next_master.shape) for v in moved]

    return (
        mixed,
        token_grad,
        grads[0][None],
        grads[1][None],
        grads[2][None],
        moved[0],
        moved[1],
        moved[2],
    )


def solution(mesh):
    fine = Mesh(
        mesh.devices.reshape(2, 4, 2, 2, 2, 16), ("x_lo", "y1", "y0", "core", "x_hi", "z")
    )
    return jax.shard_map(
        shards,
        mesh=fine,
        in_specs=(
            P(EXPERT, DP),
            P(EXPERT, DP),
            P(EXPERT, None),
            P(EXPERT, None),
            P(EXPERT, DP, None),
            P(EXPERT, DP, None),
            P(EXPERT, None, DP),
            P(EXPERT),
            P(EXPERT, DP, None),
            P(EXPERT, DP, None),
            P(EXPERT, DP, None),
        ),
        out_specs=(
            P(EXPERT, DP),
            P(EXPERT, DP),
            P(EXPERT, DP, None),
            P(EXPERT, DP, None),
            P(EXPERT, None, DP),
            P(EXPERT, DP, None),
            P(EXPERT, DP, None),
            P(EXPERT, DP, None),
        ),
        check_vma=False,
    )
```

```python
import functools

import jax
import jax.numpy as jnp
from jax import lax
from jax.experimental import pallas as pl
from jax.experimental.pallas import tpu as pltpu
from jax.sharding import Mesh
from jax.sharding import PartitionSpec as P

EXPERT = ("x_hi", "z")
DP = ("x_lo", "y1", "y0", "core")
QUAD = ("y0", "core")
SUMS = ("x_lo", "y1")
F32 = jnp.float32
BF16 = jnp.bfloat16
SWAP = [(0, 1), (1, 0)]

TOK = 64
TOP = 8
GROUPS = 32
PART = 6
QUADS = 4
ROWS = GROUPS * PART
WIDE = GROUPS * PART * QUADS
BLK = 128
FF = 768
Y = 8
NEXT = 192

PARAMS = pltpu.CompilerParams(vmem_limit_bytes=16 * 1024 * 1024)


def far(value):
    return pltpu.with_memory_space_constraint(value, pltpu.HBM)


def call(kernel, out_shape, operands, flops=0, moved=0):
    vmem = pl.BlockSpec(memory_space=pltpu.VMEM)
    smem = pl.BlockSpec(memory_space=pltpu.SMEM)
    return pl.pallas_call(
        kernel,
        out_shape=out_shape,
        in_specs=[smem if o.dtype == jnp.int32 and o.size == 1 else vmem for o in operands],
        out_specs=jax.tree.map(lambda _: vmem, out_shape, is_leaf=lambda o: hasattr(o, "shape")),
        compiler_params=PARAMS,
        cost_estimate=pl.CostEstimate(flops=flops, bytes_accessed=moved, transcendentals=0),
    )(*operands)


def row_fields(shape, dim):
    r = lax.broadcasted_iota(jnp.int32, shape, dim)
    pair = (r * 2731) >> 16
    rest = r - pair * (QUADS * PART)
    member = (rest * 43) >> 8
    return pair, member, rest - member * PART


def three(value):
    hi = value.astype(BF16)
    left = value - hi.astype(F32)
    mid = left.astype(BF16)
    return hi, mid, (left - mid.astype(F32)).astype(BF16)


def dot(a, b, dims):
    return lax.dot_general(a, b, (dims, ((), ())), preferred_element_type=F32)


def blocks_kernel(a_ref, b_ref, out_ref, sems):
    copies = []
    for d in range(QUADS):
        rows = slice(d * TOK, (d + 1) * TOK)
        copies.append(pltpu.make_async_copy(a_ref, out_ref.at[rows, :BLK], sems.at[2 * d]))
        copies.append(pltpu.make_async_copy(b_ref, out_ref.at[rows, BLK:], sems.at[2 * d + 1]))
    for copy in copies:
        copy.start()
    for copy in copies:
        copy.wait()


def blocks(a, b):
    hbm = pl.BlockSpec(memory_space=pltpu.HBM)
    return pl.pallas_call(
        blocks_kernel,
        out_shape=far_shape(QUADS * TOK, 2 * BLK),
        in_specs=[hbm, hbm],
        out_specs=hbm,
        scratch_shapes=[pltpu.SemaphoreType.DMA((2 * QUADS,))],
        compiler_params=PARAMS,
        cost_estimate=pl.CostEstimate(flops=0, bytes_accessed=262144, transcendentals=0),
    )(far(a), far(b))


def table_kernel(q_ref, routes_ref, probs_ref, prob_ref, prob_again):
    q = q_ref[0]
    shape = (TOK, WIDE)
    pair, member, slot = row_fields(shape, 1)
    chosen = jnp.zeros(shape, F32)
    weight = jnp.zeros(shape, F32)
    expert = pair.astype(F32)
    row = lax.broadcasted_iota(jnp.int32, (TOK, TOK), 0)
    col = lax.broadcasted_iota(jnp.int32, (TOK, TOK), 1)
    unit = jnp.where(col == row, 1.0, 0.0).astype(BF16)
    routes = dot(unit, routes_ref[...].astype(F32).astype(BF16), ((1,), (1,)))
    hi, mid, low = [dot(unit, part, ((1,), (1,))) for part in three(probs_ref[...])]
    probs = (hi + mid) + low
    for k in range(TOP):
        hit = routes[:, k : k + 1] == expert
        chosen = jnp.where(hit, 1.0, chosen)
        weight = jnp.where(hit, probs[:, k : k + 1], weight)
    before = jnp.where(col < row, 1.0, 0.0).astype(BF16)
    position = dot(before, chosen.astype(BF16), ((1,), (0,)))
    here = (chosen > 0.5) & (position == (q * PART + slot).astype(F32))
    prob = jnp.where(here, weight, 0.0)
    prob_ref[...] = prob
    prob_again[...] = prob


def dispatch_kernel(q_ref, prob_ref, tok_ref, pay_ref):
    shape = (TOK, WIDE)
    _, member, _ = row_fields(shape, 1)
    prob = prob_ref[...]
    mask = jnp.where(prob > 0.0, 1.0, 0.0)
    masks = [jnp.where(member == d, mask, 0.0).astype(BF16) for d in range(QUADS)]
    parts = three(prob)
    x = jnp.zeros((WIDE, BLK), F32)
    dy = jnp.zeros((WIDE, BLK), F32)
    zero = jnp.zeros(shape, BF16)
    for d in range(QUADS):
        rows = pl.ds(pl.multiple_of((q_ref[0] ^ d) * TOK, TOK), TOK)
        x_tok = tok_ref[rows, :BLK]
        dy_tok = tok_ref[rows, BLK:]
        x = x + dot(masks[d], x_tok, ((0,), (0,)))
        for part in parts:
            dy = dy + dot(jnp.where(member == d, part, zero), dy_tok, ((0,), (0,)))
    pay_ref[:, :BLK] = x.astype(BF16)
    pay_ref[:, BLK:] = dy.astype(BF16)


def place(d):
    i = lax.broadcasted_iota(jnp.int32, (ROWS, WIDE), 0)
    r = lax.broadcasted_iota(jnp.int32, (ROWS, WIDE), 1)
    group = (i * 10923) >> 16
    want = group * (QUADS * PART) + d * PART + (i - group * PART)
    return jnp.where(r == want, 1.0, 0.0).astype(BF16)


def partial_kernel(pay_ref, w0, w1, w2, w3, sums_hbm, x_hbm, dy_hbm, sums_ref, rows_ref, sems):
    got = pay_ref[...]
    for d in range(QUADS):
        moved = dot(place(d), got, ((1,), (0,))).astype(BF16)
        rows_ref[0, :, d * BLK : (d + 1) * BLK] = moved[:, :BLK]
        rows_ref[1, :, d * BLK : (d + 1) * BLK] = moved[:, BLK:]
    copies = [
        pltpu.make_async_copy(rows_ref.at[0], x_hbm, sems.at[3]),
        pltpu.make_async_copy(rows_ref.at[1], dy_hbm, sems.at[4]),
    ]
    for k in range(3):
        rows = rows_ref[k // 2]
        low = jnp.concatenate([w0[k], w1[k]], axis=0)
        high = jnp.concatenate([w2[k], w3[k]], axis=0)
        total = dot(rows[:, : 2 * BLK], low, ((1,), (0,))) + dot(
            rows[:, 2 * BLK :], high, ((1,), (0,))
        )
        at = slice(k * FF, (k + 1) * FF)
        sums_ref[:, at] = total.astype(BF16)
        copies.append(pltpu.make_async_copy(sums_ref.at[:, at], sums_hbm.at[:, at], sems.at[k]))
        copies[-1].start()
    copies[0].start()
    copies[1].start()
    for copy in copies:
        copy.wait()


def partial_sums(*operands):
    vmem, hbm = [pl.BlockSpec(memory_space=m) for m in (pltpu.VMEM, pltpu.HBM)]
    return pl.pallas_call(
        partial_kernel,
        out_shape=(far_shape(ROWS, 3 * FF), far_shape(ROWS, 4 * BLK), far_shape(ROWS, 4 * BLK)),
        in_specs=[vmem] * 5,
        out_specs=[hbm] * 3,
        scratch_shapes=[
            pltpu.VMEM((ROWS, 3 * FF), BF16),
            pltpu.VMEM((2, ROWS, 4 * BLK), BF16),
            pltpu.SemaphoreType.DMA((5,)),
        ],
        compiler_params=PARAMS,
        cost_estimate=pl.CostEstimate(
            flops=2 * 3 * ROWS * FF * 4 * BLK, bytes_accessed=4000000, transcendentals=0
        ),
    )(*operands)


def act_kernel(in_ref, out_ref):
    rows = ROWS // Y
    for lo in range(0, FF, 256):
        vals = []
        for k in range(3):
            block = in_ref[:, k * FF + lo : k * FF + lo + 256].astype(F32)
            total = block[:rows]
            for y in range(1, Y):
                total = total + block[y * rows : (y + 1) * rows]
            vals.append(total)
        gate, up, back = vals
        s = jax.nn.sigmoid(gate)
        act = gate * s * up
        grad_g = back * up * s * (1.0 + gate * (1.0 - s))
        grad_u = back * gate * s
        for k, value in enumerate((act, grad_g, grad_u)):
            at = slice(k * FF + lo, k * FF + lo + 256)
            out_ref[:, at] = jnp.concatenate([value] * Y, axis=0).astype(BF16)


def back_kernel(h_ref, w0, w1, w2, w3, pay_ref):
    act = h_ref[:, :FF]
    grad_g = h_ref[:, FF : 2 * FF]
    grad_u = h_ref[:, 2 * FF :]
    pair, member, slot = row_fields((WIDE, ROWS), 0)
    source = member * ROWS + pair * PART + slot
    col = lax.broadcasted_iota(jnp.int32, (WIDE, ROWS), 1)
    total = jnp.zeros((WIDE, 2 * BLK), F32)
    for p, (wa, wb) in enumerate(((w0, w1), (w2, w3))):
        weights = [jnp.concatenate([wa[k], wb[k]], axis=0) for k in range(3)]
        y = dot(act, weights[2], ((1,), (1,))).astype(BF16)
        dx = dot(grad_g, weights[0], ((1,), (1,))) + dot(grad_u, weights[1], ((1,), (1,)))
        dx = dx.astype(BF16)
        for h in range(2):
            both = jnp.concatenate([v[:, h * BLK : (h + 1) * BLK] for v in (y, dx)], axis=1)
            onehot = jnp.where(source == col + (2 * p + h) * ROWS, 1.0, 0.0).astype(BF16)
            total = total + dot(onehot, both, ((1,), (0,)))
    pay_ref[...] = total.astype(BF16)


def grad_kernel(h_ref, x_ref, dy_ref, keep_ref, send_ref):
    for d in range(QUADS):
        for k in range(3):
            rows_ref = dy_ref if k == 2 else x_ref
            h_at = (FF, 2 * FF, 0)[k]
            part = dot(
                rows_ref[:, d * BLK : (d + 1) * BLK], h_ref[:, h_at : h_at + FF], ((0,), (0,))
            )
            if d % 2:
                send_ref[d // 2, k] = part.astype(BF16)
            else:
                keep_ref[d // 2, k] = part


def add_near_kernel(keep_ref, near_ref, kept_ref, passed_ref):
    for k in range(3):
        kept_ref[k] = keep_ref[0, k] + near_ref[0, k].astype(F32)
        passed_ref[k] = (keep_ref[1, k] + near_ref[1, k].astype(F32)).astype(BF16)


def add_far_kernel(kept_ref, other_ref, gate_ref, up_ref, down_ref):
    gate_ref[...] = (kept_ref[0] + other_ref[0].astype(F32)).astype(BF16)
    up_ref[...] = (kept_ref[1] + other_ref[1].astype(F32)).astype(BF16)
    down_ref[...] = (kept_ref[2] + other_ref[2].astype(F32)).T.astype(BF16)


def combine_kernel(q_ref, pay_ref, prob_ref, out_ref):
    q = q_ref[0]
    shape = (TOK, WIDE)
    _, member, _ = row_fields(shape, 1)
    y = pay_ref[:, :BLK]
    dx = pay_ref[:, BLK:]
    prob = prob_ref[...]
    mask = jnp.where(prob > 0.0, 1.0, 0.0)
    for d in range(QUADS):
        at = member == d
        mixed = jnp.zeros((TOK, BLK), F32)
        for part in three(jnp.where(at, prob, 0.0)):
            mixed = mixed + dot(part, y, ((1,), (0,)))
        grad = dot(jnp.where(at, mask, 0.0).astype(BF16), dx, ((1,), (0,)))
        out_ref[q ^ d] = jnp.concatenate([mixed, grad], axis=1).astype(BF16)


def stack_kernel(a_ref, b_ref, c_ref, low_ref, high_ref):
    half = NEXT // 2
    low_ref[:NEXT] = a_ref[...]
    low_ref[NEXT:] = b_ref[:half]
    high_ref[:half] = b_ref[half:]
    high_ref[half:] = c_ref[...]


def select_kernel(moving_ref, low_new, high_new, low_old, high_old, a_ref, b_ref, c_ref):
    half = NEXT // 2
    moving = moving_ref[0] != 0
    low = jnp.where(moving, low_new[...], low_old[...])
    high = jnp.where(moving, high_new[...], high_old[...])
    a_ref[...] = low[:NEXT]
    b_ref[:half] = low[NEXT:]
    b_ref[half:] = high[:half]
    c_ref[...] = high[half:]


def shape_of(*dims, dtype=BF16):
    return jax.ShapeDtypeStruct(dims, dtype)


def far_shape(*dims, dtype=BF16):
    return pltpu.HBM(dims, dtype)


def shards(
    tokens,
    grad_out,
    routes,
    gate_probs,
    w_gate,
    w_up,
    w_down,
    dest,
    next_master,
    next_first,
    next_second,
):
    quad = (lax.axis_index("y0") * 2 + lax.axis_index("core")).astype(jnp.int32).reshape(1)

    with jax.named_scope("tokens_to_quad"):
        shared = lax.all_to_all(
            blocks(tokens, grad_out), QUAD, split_axis=0, concat_axis=0, tiled=True
        )

    with jax.named_scope("weights_to_quad"):
        w0 = jnp.stack([w_gate[0], w_up[0], w_down[0].T])
        w2 = lax.ppermute(w0, "y0", SWAP)
        w1 = lax.ppermute(w0, "core", SWAP)
        w3 = lax.ppermute(w2, "core", SWAP)

    with jax.named_scope("dispatch"):
        prob, prob_again = call(
            table_kernel,
            (shape_of(TOK, WIDE, dtype=F32), far_shape(TOK, WIDE, dtype=F32)),
            (quad, far(routes.T), far(gate_probs.T)),
            flops=2 * TOK * TOK * WIDE,
            moved=300000,
        )
        pay = call(
            dispatch_kernel,
            shape_of(WIDE, 2 * BLK),
            (quad, prob, shared),
            flops=2 * 16 * TOK * WIDE * BLK,
            moved=800000,
        )
        got = lax.all_to_all(pay, EXPERT, split_axis=0, concat_axis=0, tiled=True)

    with jax.named_scope("relocate"):
        mine_next = [v.reshape(NEXT, BLK) for v in (next_master, next_first, next_second)]
        halves = [shape_of(3 * NEXT // 2, BLK, dtype=F32)] * 2
        low, high = call(stack_kernel, halves, mine_next, moved=600000)

    with jax.named_scope("partial_sums"):
        sums, x_rows, dy_rows = partial_sums(got, w0, w1, w2, w3)
        sums, low = lax.optimization_barrier((sums, low))
        parts = lax.all_to_all(sums, SUMS, split_axis=0, concat_axis=0, tiled=True)
        low_new = lax.ppermute(low, "x_hi", SWAP)
        parts, low_new = lax.optimization_barrier((parts, low_new))

    with jax.named_scope("activation"):
        hidden = call(
            act_kernel, far_shape(ROWS, 3 * FF), (parts,), flops=4000000, moved=1000000
        )
        hidden, high = lax.optimization_barrier((hidden, high))
        whole = lax.all_to_all(hidden, SUMS, split_axis=0, concat_axis=0, tiled=True)
        high_new = lax.ppermute(high, "x_hi", SWAP)
        whole, high_new = lax.optimization_barrier((whole, high_new))

    with jax.named_scope("slot_outputs"):
        back = call(
            back_kernel,
            far_shape(WIDE, 2 * BLK),
            (whole, w0, w1, w2, w3),
            flops=2 * 3 * ROWS * FF * 4 * BLK,
            moved=4000000,
        )
        back, whole = lax.optimization_barrier((back, whole))
        returned = lax.all_to_all(back, EXPERT, split_axis=0, concat_axis=0, tiled=True)

    with jax.named_scope("relocate"):
        moving = (dest != lax.axis_index(EXPERT).astype(jnp.int32)).astype(jnp.int32)
        moved = call(
            select_kernel,
            [far_shape(NEXT, BLK, dtype=F32)] * 3,
            (moving, low_new, high_new, low, high),
            moved=1200000,
        )

    with jax.named_scope("weight_grads"):
        keep, send = call(
            grad_kernel,
            (shape_of(2, 3, BLK, FF, dtype=F32), shape_of(2, 3, BLK, FF)),
            (whole, x_rows, dy_rows),
            flops=40 * 3 * ROWS * FF * 4 * BLK,
            moved=100000000,
        )
        near_part = lax.ppermute(send, "core", SWAP)
        kept, passed = call(
            add_near_kernel,
            (far_shape(3, BLK, FF, dtype=F32), shape_of(3, BLK, FF)),
            (keep, near_part),
        )
        passed, moved = lax.optimization_barrier((passed, moved))
        other = lax.ppermute(passed, "y0", SWAP)
        grads = call(
            add_far_kernel,
            (far_shape(BLK, FF), far_shape(BLK, FF), far_shape(FF, BLK)),
            (kept, other),
            flops=300000,
            moved=3000000,
        )

    with jax.named_scope("combine"):
        mixes = call(
            combine_kernel,
            shape_of(QUADS, TOK, 2 * BLK),
            (quad, returned, far(prob_again)),
            flops=2 * 16 * TOK * WIDE * BLK,
            moved=800000,
        )
        mixes = lax.all_to_all(mixes, QUAD, split_axis=0, concat_axis=0, tiled=True)
        mixes = jnp.sum(mixes.astype(F32), axis=0).astype(BF16)
        mixed, token_grad = mixes[:, :BLK], mixes[:, BLK:]

    return (
        mixed,
        token_grad,
        grads[0][None],
        grads[1][None],
        grads[2][None],
        *[v.reshape(next_master.shape) for v in moved],
    )


def solution(mesh):
    fine = Mesh(
        mesh.devices.reshape(2, 4, 2, 2, 2, 16), ("x_lo", "y1", "y0", "core", "x_hi", "z")
    )
    return jax.shard_map(
        shards,
        mesh=fine,
        in_specs=(
            P(EXPERT, DP),
            P(EXPERT, DP),
            P(EXPERT, None),
            P(EXPERT, None),
            P(EXPERT, DP, None),
            P(EXPERT, DP, None),
            P(EXPERT, None, DP),
            P(EXPERT),
            P(EXPERT, DP, None),
            P(EXPERT, DP, None),
            P(EXPERT, DP, None),
        ),
        out_specs=(
            P(EXPERT, DP),
            P(EXPERT, DP),
            P(EXPERT, DP, None),
            P(EXPERT, DP, None),
            P(EXPERT, None, DP),
            P(EXPERT, DP, None),
            P(EXPERT, DP, None),
            P(EXPERT, DP, None),
        ),
        check_vma=False,
    )
```

```python
import functools

import jax
import jax.numpy as jnp
from jax import lax
from jax.experimental import pallas as pl
from jax.experimental.pallas import tpu as pltpu
from jax.sharding import Mesh
from jax.sharding import PartitionSpec as P

EXPERT = ("x_hi", "z")
DP = ("x_lo", "y1", "y0", "core")
QUAD = ("y0", "core")
SUMS = ("x_lo", "y1")
F32 = jnp.float32
BF16 = jnp.bfloat16
SWAP = [(0, 1), (1, 0)]

TOK = 64
TOP = 8
GROUPS = 32
PART = 6
QUADS = 4
ROWS = GROUPS * PART
WIDE = GROUPS * PART * QUADS
BLK = 128
FF = 768
Y = 8
NEXT = 192

PARAMS = pltpu.CompilerParams(vmem_limit_bytes=16 * 1024 * 1024)


def far(value):
    return pltpu.with_memory_space_constraint(value, pltpu.HBM)


def call(kernel, out_shape, operands, flops=0, moved=0):
    vmem = pl.BlockSpec(memory_space=pltpu.VMEM)
    smem = pl.BlockSpec(memory_space=pltpu.SMEM)
    return pl.pallas_call(
        kernel,
        out_shape=out_shape,
        in_specs=[smem if o.dtype == jnp.int32 and o.size == 1 else vmem for o in operands],
        out_specs=jax.tree.map(lambda _: vmem, out_shape, is_leaf=lambda o: hasattr(o, "shape")),
        compiler_params=PARAMS,
        cost_estimate=pl.CostEstimate(flops=flops, bytes_accessed=moved, transcendentals=0),
    )(*operands)


def row_fields(shape, dim):
    r = lax.broadcasted_iota(jnp.int32, shape, dim)
    pair = (r * 2731) >> 16
    rest = r - pair * (QUADS * PART)
    member = (rest * 43) >> 8
    return pair, member, rest - member * PART


def three(value):
    hi = value.astype(BF16)
    left = value - hi.astype(F32)
    mid = left.astype(BF16)
    return hi, mid, (left - mid.astype(F32)).astype(BF16)


def dot(a, b, dims):
    return lax.dot_general(a, b, (dims, ((), ())), preferred_element_type=F32)


def blocks_kernel(a_ref, b_ref, out_ref):
    both = jnp.concatenate([a_ref[...], b_ref[...]], axis=1)
    for d in range(QUADS):
        out_ref[d * TOK : (d + 1) * TOK] = both


def table_kernel(q_ref, routes_ref, probs_ref, prob_ref, prob_again):
    q = q_ref[0]
    shape = (TOK, WIDE)
    pair, member, slot = row_fields(shape, 1)
    chosen = jnp.zeros(shape, F32)
    weight = jnp.zeros(shape, F32)
    expert = pair.astype(F32)
    row = lax.broadcasted_iota(jnp.int32, (TOK, TOK), 0)
    col = lax.broadcasted_iota(jnp.int32, (TOK, TOK), 1)
    unit = jnp.where(col == row, 1.0, 0.0).astype(BF16)
    routes = dot(unit, routes_ref[...].astype(F32).astype(BF16), ((1,), (1,)))
    hi, mid, low = [dot(unit, part, ((1,), (1,))) for part in three(probs_ref[...])]
    probs = (hi + mid) + low
    for k in range(TOP):
        hit = routes[:, k : k + 1] == expert
        chosen = jnp.where(hit, 1.0, chosen)
        weight = jnp.where(hit, probs[:, k : k + 1], weight)
    before = jnp.where(col < row, 1.0, 0.0).astype(BF16)
    position = dot(before, chosen.astype(BF16), ((1,), (0,)))
    here = (chosen > 0.5) & (position == (q * PART + slot).astype(F32))
    prob = jnp.where(here, weight, 0.0)
    prob_ref[...] = prob
    prob_again[...] = prob


def dispatch_kernel(q_ref, prob_ref, tok_ref, pay_ref):
    shape = (TOK, WIDE)
    _, member, _ = row_fields(shape, 1)
    prob = prob_ref[...]
    mask = jnp.where(prob > 0.0, 1.0, 0.0)
    masks = [jnp.where(member == d, mask, 0.0).astype(BF16) for d in range(QUADS)]
    parts = three(prob)
    x = jnp.zeros((WIDE, BLK), F32)
    dy = jnp.zeros((WIDE, BLK), F32)
    zero = jnp.zeros(shape, BF16)
    for d in range(QUADS):
        rows = pl.ds(pl.multiple_of((q_ref[0] ^ d) * TOK, TOK), TOK)
        x_tok = tok_ref[rows, :BLK]
        dy_tok = tok_ref[rows, BLK:]
        x = x + dot(masks[d], x_tok, ((0,), (0,)))
        for part in parts:
            dy = dy + dot(jnp.where(member == d, part, zero), dy_tok, ((0,), (0,)))
    pay_ref[:, :BLK] = x.astype(BF16)
    pay_ref[:, BLK:] = dy.astype(BF16)


def place(d):
    i = lax.broadcasted_iota(jnp.int32, (ROWS, WIDE), 0)
    r = lax.broadcasted_iota(jnp.int32, (ROWS, WIDE), 1)
    group = (i * 10923) >> 16
    want = group * (QUADS * PART) + d * PART + (i - group * PART)
    return jnp.where(r == want, 1.0, 0.0).astype(BF16)


def partial_kernel(pay_ref, w0, w1, w2, w3, sums_hbm, x_hbm, dy_hbm, sums_ref, rows_ref, sems):
    got = pay_ref[...]
    for d in range(QUADS):
        moved = dot(place(d), got, ((1,), (0,))).astype(BF16)
        rows_ref[0, :, d * BLK : (d + 1) * BLK] = moved[:, :BLK]
        rows_ref[1, :, d * BLK : (d + 1) * BLK] = moved[:, BLK:]
    copies = [
        pltpu.make_async_copy(rows_ref.at[0], x_hbm, sems.at[3]),
        pltpu.make_async_copy(rows_ref.at[1], dy_hbm, sems.at[4]),
    ]
    for k in range(3):
        rows = rows_ref[k // 2]
        low = jnp.concatenate([w0[k], w1[k]], axis=0)
        high = jnp.concatenate([w2[k], w3[k]], axis=0)
        total = dot(rows[:, : 2 * BLK], low, ((1,), (0,))) + dot(
            rows[:, 2 * BLK :], high, ((1,), (0,))
        )
        at = slice(k * FF, (k + 1) * FF)
        sums_ref[:, at] = total.astype(BF16)
        copies.append(pltpu.make_async_copy(sums_ref.at[:, at], sums_hbm.at[:, at], sems.at[k]))
        copies[-1].start()
    copies[0].start()
    copies[1].start()
    for copy in copies:
        copy.wait()


def partial_sums(*operands):
    vmem, hbm = [pl.BlockSpec(memory_space=m) for m in (pltpu.VMEM, pltpu.HBM)]
    return pl.pallas_call(
        partial_kernel,
        out_shape=(far_shape(ROWS, 3 * FF), far_shape(ROWS, 4 * BLK), far_shape(ROWS, 4 * BLK)),
        in_specs=[vmem] * 5,
        out_specs=[hbm] * 3,
        scratch_shapes=[
            pltpu.VMEM((ROWS, 3 * FF), BF16),
            pltpu.VMEM((2, ROWS, 4 * BLK), BF16),
            pltpu.SemaphoreType.DMA((5,)),
        ],
        compiler_params=PARAMS,
        cost_estimate=pl.CostEstimate(
            flops=2 * 3 * ROWS * FF * 4 * BLK, bytes_accessed=4000000, transcendentals=0
        ),
    )(*operands)


def act_kernel(in_ref, out_ref):
    rows = ROWS // Y
    for lo in range(0, FF, 256):
        vals = []
        for k in range(3):
            block = in_ref[:, k * FF + lo : k * FF + lo + 256].astype(F32)
            total = block[:rows]
            for y in range(1, Y):
                total = total + block[y * rows : (y + 1) * rows]
            vals.append(total)
        gate, up, back = vals
        s = jax.nn.sigmoid(gate)
        act = gate * s * up
        grad_g = back * up * s * (1.0 + gate * (1.0 - s))
        grad_u = back * gate * s
        for k, value in enumerate((act, grad_g, grad_u)):
            at = slice(k * FF + lo, k * FF + lo + 256)
            out_ref[:, at] = jnp.concatenate([value] * Y, axis=0).astype(BF16)


def back_kernel(h_ref, w0, w1, w2, w3, pay_ref):
    act = h_ref[:, :FF]
    grad_g = h_ref[:, FF : 2 * FF]
    grad_u = h_ref[:, 2 * FF :]
    pair, member, slot = row_fields((WIDE, ROWS), 0)
    source = member * ROWS + pair * PART + slot
    col = lax.broadcasted_iota(jnp.int32, (WIDE, ROWS), 1)
    total = jnp.zeros((WIDE, 2 * BLK), F32)
    for p, (wa, wb) in enumerate(((w0, w1), (w2, w3))):
        weights = [jnp.concatenate([wa[k], wb[k]], axis=0) for k in range(3)]
        y = dot(act, weights[2], ((1,), (1,))).astype(BF16)
        dx = dot(grad_g, weights[0], ((1,), (1,))) + dot(grad_u, weights[1], ((1,), (1,)))
        dx = dx.astype(BF16)
        for h in range(2):
            both = jnp.concatenate([v[:, h * BLK : (h + 1) * BLK] for v in (y, dx)], axis=1)
            onehot = jnp.where(source == col + (2 * p + h) * ROWS, 1.0, 0.0).astype(BF16)
            total = total + dot(onehot, both, ((1,), (0,)))
    pay_ref[...] = total.astype(BF16)


def grad_kernel(h_ref, x_ref, dy_ref, keep_ref, send_ref):
    for d in range(QUADS):
        for k in range(3):
            rows_ref = dy_ref if k == 2 else x_ref
            h_at = (FF, 2 * FF, 0)[k]
            part = dot(
                rows_ref[:, d * BLK : (d + 1) * BLK], h_ref[:, h_at : h_at + FF], ((0,), (0,))
            )
            if d % 2:
                send_ref[d // 2, k] = part.astype(BF16)
            else:
                keep_ref[d // 2, k] = part


def add_near_kernel(keep_ref, near_ref, kept_ref, passed_ref):
    for k in range(3):
        kept_ref[k] = keep_ref[0, k] + near_ref[0, k].astype(F32)
        passed_ref[k] = (keep_ref[1, k] + near_ref[1, k].astype(F32)).astype(BF16)


def add_far_kernel(kept_ref, other_ref, gate_ref, up_ref, down_ref):
    gate_ref[...] = (kept_ref[0] + other_ref[0].astype(F32)).astype(BF16)
    up_ref[...] = (kept_ref[1] + other_ref[1].astype(F32)).astype(BF16)
    down_ref[...] = (kept_ref[2] + other_ref[2].astype(F32)).T.astype(BF16)


def combine_kernel(q_ref, pay_ref, prob_ref, out_ref):
    q = q_ref[0]
    shape = (TOK, WIDE)
    _, member, _ = row_fields(shape, 1)
    y = pay_ref[:, :BLK]
    dx = pay_ref[:, BLK:]
    prob = prob_ref[...]
    mask = jnp.where(prob > 0.0, 1.0, 0.0)
    for d in range(QUADS):
        at = member == d
        mixed = jnp.zeros((TOK, BLK), F32)
        for part in three(jnp.where(at, prob, 0.0)):
            mixed = mixed + dot(part, y, ((1,), (0,)))
        grad = dot(jnp.where(at, mask, 0.0).astype(BF16), dx, ((1,), (0,)))
        out_ref[q ^ d] = jnp.concatenate([mixed, grad], axis=1).astype(BF16)


def stack_kernel(a_ref, b_ref, c_ref, out_ref):
    for k, ref in enumerate((a_ref, b_ref, c_ref)):
        out_ref[k * NEXT : (k + 1) * NEXT] = ref[...]


def select_kernel(moving_ref, partner_ref, state_ref, a_ref, b_ref, c_ref):
    moving = moving_ref[0] != 0
    for k, ref in enumerate((a_ref, b_ref, c_ref)):
        rows = slice(k * NEXT, (k + 1) * NEXT)
        ref[...] = jnp.where(moving, partner_ref[rows], state_ref[rows])


def shape_of(*dims, dtype=BF16):
    return jax.ShapeDtypeStruct(dims, dtype)


def far_shape(*dims, dtype=BF16):
    return pltpu.HBM(dims, dtype)


def shards(
    tokens,
    grad_out,
    routes,
    gate_probs,
    w_gate,
    w_up,
    w_down,
    dest,
    next_master,
    next_first,
    next_second,
):
    quad = (lax.axis_index("y0") * 2 + lax.axis_index("core")).astype(jnp.int32).reshape(1)

    with jax.named_scope("tokens_to_quad"):
        shared = lax.all_to_all(
            call(
                blocks_kernel,
                far_shape(QUADS * TOK, 2 * BLK),
                (far(tokens), far(grad_out)),
                moved=200000,
            ),
            QUAD,
            split_axis=0,
            concat_axis=0,
            tiled=True,
        )

    with jax.named_scope("relocate"):
        mine_next = [v.reshape(NEXT, BLK) for v in (next_master, next_first, next_second)]
        state = call(stack_kernel, shape_of(3 * NEXT, BLK, dtype=F32), mine_next, moved=600000)
        partner = lax.ppermute(state, "x_hi", SWAP)

    with jax.named_scope("weights_to_quad"):
        w0 = jnp.stack([w_gate[0], w_up[0], w_down[0].T])
        w2 = lax.ppermute(w0, "y0", SWAP)
        w1 = lax.ppermute(w0, "core", SWAP)
        w2, partner, state = lax.optimization_barrier((w2, partner, state))
        w3 = lax.ppermute(w2, "core", SWAP)

    with jax.named_scope("dispatch"):
        prob, prob_again = call(
            table_kernel,
            (shape_of(TOK, WIDE, dtype=F32), far_shape(TOK, WIDE, dtype=F32)),
            (quad, far(routes.T), far(gate_probs.T)),
            flops=2 * TOK * TOK * WIDE,
            moved=300000,
        )
        pay = call(
            dispatch_kernel,
            shape_of(WIDE, 2 * BLK),
            (quad, prob, shared),
            flops=2 * 16 * TOK * WIDE * BLK,
            moved=800000,
        )
        got = lax.all_to_all(pay, EXPERT, split_axis=0, concat_axis=0, tiled=True)

    with jax.named_scope("partial_sums"):
        sums, x_rows, dy_rows = partial_sums(got, w0, w1, w2, w3)
        parts = lax.all_to_all(sums, SUMS, split_axis=0, concat_axis=0, tiled=True)

    with jax.named_scope("activation"):
        hidden = call(
            act_kernel, far_shape(ROWS, 3 * FF), (parts,), flops=4000000, moved=1000000
        )
        whole = lax.all_to_all(hidden, SUMS, split_axis=0, concat_axis=0, tiled=True)

    with jax.named_scope("slot_outputs"):
        back = call(
            back_kernel,
            far_shape(WIDE, 2 * BLK),
            (whole, w0, w1, w2, w3),
            flops=2 * 3 * ROWS * FF * 4 * BLK,
            moved=4000000,
        )
        back, whole = lax.optimization_barrier((back, whole))
        returned = lax.all_to_all(back, EXPERT, split_axis=0, concat_axis=0, tiled=True)

    with jax.named_scope("relocate"):
        moving = (dest != lax.axis_index(EXPERT).astype(jnp.int32)).astype(jnp.int32)
        moved = call(
            select_kernel,
            [far_shape(NEXT, BLK, dtype=F32)] * 3,
            (moving, partner, state),
            moved=1200000,
        )

    with jax.named_scope("weight_grads"):
        keep, send = call(
            grad_kernel,
            (shape_of(2, 3, BLK, FF, dtype=F32), shape_of(2, 3, BLK, FF)),
            (whole, x_rows, dy_rows),
            flops=40 * 3 * ROWS * FF * 4 * BLK,
            moved=100000000,
        )
        near_part = lax.ppermute(send, "core", SWAP)
        kept, passed = call(
            add_near_kernel,
            (far_shape(3, BLK, FF, dtype=F32), shape_of(3, BLK, FF)),
            (keep, near_part),
        )
        passed, moved = lax.optimization_barrier((passed, moved))
        other = lax.ppermute(passed, "y0", SWAP)
        grads = call(
            add_far_kernel,
            (far_shape(BLK, FF), far_shape(BLK, FF), far_shape(FF, BLK)),
            (kept, other),
            flops=300000,
            moved=3000000,
        )

    with jax.named_scope("combine"):
        mixes = call(
            combine_kernel,
            shape_of(QUADS, TOK, 2 * BLK),
            (quad, returned, far(prob_again)),
            flops=2 * 16 * TOK * WIDE * BLK,
            moved=800000,
        )
        mixes = lax.all_to_all(mixes, QUAD, split_axis=0, concat_axis=0, tiled=True)
        mixes = jnp.sum(mixes.astype(F32), axis=0).astype(BF16)
        mixed, token_grad = mixes[:, :BLK], mixes[:, BLK:]

    return (
        mixed,
        token_grad,
        grads[0][None],
        grads[1][None],
        grads[2][None],
        *[v.reshape(next_master.shape) for v in moved],
    )


def solution(mesh):
    fine = Mesh(
        mesh.devices.reshape(2, 4, 2, 2, 2, 16), ("x_lo", "y1", "y0", "core", "x_hi", "z")
    )
    return jax.shard_map(
        shards,
        mesh=fine,
        in_specs=(
            P(EXPERT, DP),
            P(EXPERT, DP),
            P(EXPERT, None),
            P(EXPERT, None),
            P(EXPERT, DP, None),
            P(EXPERT, DP, None),
            P(EXPERT, None, DP),
            P(EXPERT),
            P(EXPERT, DP, None),
            P(EXPERT, DP, None),
            P(EXPERT, DP, None),
        ),
        out_specs=(
            P(EXPERT, DP),
            P(EXPERT, DP),
            P(EXPERT, DP, None),
            P(EXPERT, DP, None),
            P(EXPERT, None, DP),
            P(EXPERT, DP, None),
            P(EXPERT, DP, None),
            P(EXPERT, DP, None),
        ),
        check_vma=False,
    )
```

```python
import functools

import jax
import jax.numpy as jnp
from jax import lax
from jax.experimental import pallas as pl
from jax.experimental.pallas import tpu as pltpu
from jax.sharding import Mesh
from jax.sharding import PartitionSpec as P

EXPERT = ("x_hi", "z")
DP = ("x_lo", "y1", "y0", "core")
QUAD = ("y0", "core")
SUMS = ("x_lo", "y1")
F32 = jnp.float32
BF16 = jnp.bfloat16
SWAP = [(0, 1), (1, 0)]

TOK = 64
TOP = 8
GROUPS = 32
PART = 6
QUADS = 4
ROWS = GROUPS * PART
WIDE = GROUPS * PART * QUADS
BLK = 128
FF = 768
Y = 8
NEXT = 192

PARAMS = pltpu.CompilerParams(vmem_limit_bytes=16 * 1024 * 1024)


def far(value):
    return pltpu.with_memory_space_constraint(value, pltpu.HBM)


def call(kernel, out_shape, operands, flops=0, moved=0):
    vmem = pl.BlockSpec(memory_space=pltpu.VMEM)
    smem = pl.BlockSpec(memory_space=pltpu.SMEM)
    return pl.pallas_call(
        kernel,
        out_shape=out_shape,
        in_specs=[smem if o.dtype == jnp.int32 and o.size == 1 else vmem for o in operands],
        out_specs=jax.tree.map(lambda _: vmem, out_shape, is_leaf=lambda o: hasattr(o, "shape")),
        compiler_params=PARAMS,
        cost_estimate=pl.CostEstimate(flops=flops, bytes_accessed=moved, transcendentals=0),
    )(*operands)


def row_fields(shape, dim):
    r = lax.broadcasted_iota(jnp.int32, shape, dim)
    pair = (r * 2731) >> 16
    rest = r - pair * (QUADS * PART)
    member = (rest * 43) >> 8
    return pair, member, rest - member * PART


def three(value):
    hi = value.astype(BF16)
    left = value - hi.astype(F32)
    mid = left.astype(BF16)
    return hi, mid, (left - mid.astype(F32)).astype(BF16)


def dot(a, b, dims):
    return lax.dot_general(a, b, (dims, ((), ())), preferred_element_type=F32)


def blocks_kernel(a_ref, b_ref, out_ref):
    both = jnp.concatenate([a_ref[...], b_ref[...]], axis=1)
    for d in range(QUADS):
        out_ref[d * TOK : (d + 1) * TOK] = both


def table_kernel(q_ref, routes_ref, probs_ref, prob_ref, prob_again):
    q = q_ref[0]
    shape = (TOK, WIDE)
    pair, member, slot = row_fields(shape, 1)
    chosen = jnp.zeros(shape, F32)
    weight = jnp.zeros(shape, F32)
    expert = pair.astype(F32)
    row = lax.broadcasted_iota(jnp.int32, (TOK, TOK), 0)
    col = lax.broadcasted_iota(jnp.int32, (TOK, TOK), 1)
    unit = jnp.where(col == row, 1.0, 0.0).astype(BF16)
    routes = dot(unit, routes_ref[...].astype(F32).astype(BF16), ((1,), (1,)))
    hi, mid, low = [dot(unit, part, ((1,), (1,))) for part in three(probs_ref[...])]
    probs = (hi + mid) + low
    for k in range(TOP):
        hit = routes[:, k : k + 1] == expert
        chosen = jnp.where(hit, 1.0, chosen)
        weight = jnp.where(hit, probs[:, k : k + 1], weight)
    before = jnp.where(col < row, 1.0, 0.0).astype(BF16)
    position = dot(before, chosen.astype(BF16), ((1,), (0,)))
    here = (chosen > 0.5) & (position == (q * PART + slot).astype(F32))
    prob = jnp.where(here, weight, 0.0)
    prob_ref[...] = prob
    prob_again[...] = prob


def stacked(value, q):
    _, member, _ = row_fields(value.shape, 1)
    own = member ^ q
    return jnp.concatenate([jnp.where(own == m, value, 0.0) for m in range(QUADS)], axis=0)


def dispatch_kernel(q_ref, prob_ref, tok_ref, pay_ref):
    prob = stacked(prob_ref[...], q_ref[0])
    mask = jnp.where(prob > 0.0, 1.0, 0.0).astype(BF16)
    pay_ref[:, :BLK] = dot(mask, tok_ref[:, :BLK], ((0,), (0,))).astype(BF16)
    parts = jnp.concatenate(three(prob), axis=0)
    cotangents = jnp.concatenate([tok_ref[:, BLK:]] * 3, axis=0)
    pay_ref[:, BLK:] = dot(parts, cotangents, ((0,), (0,))).astype(BF16)


def equal_to(want, width):
    lane = lax.broadcasted_iota(jnp.int32, want.shape, 1)
    return jnp.concatenate(
        [jnp.where(want == lane + at, 1.0, 0.0).astype(BF16) for at in range(0, width, BLK)],
        axis=1,
    )


def place():
    i = lax.broadcasted_iota(jnp.int32, (ROWS, BLK), 0)
    group = (i * 10923) >> 16
    first = group * (QUADS * PART) + (i - group * PART)
    return jnp.concatenate([equal_to(first + d * PART, WIDE) for d in range(QUADS)], axis=0)


def partial_kernel(pay_ref, w0, w1, w2, w3, sums_hbm, x_hbm, dy_hbm, sums_ref, rows_ref, sems):
    moved = dot(place(), pay_ref[...], ((1,), (0,))).astype(BF16)
    for d in range(QUADS):
        block = moved[d * ROWS : (d + 1) * ROWS]
        rows_ref[0, :, d * BLK : (d + 1) * BLK] = block[:, :BLK]
        rows_ref[1, :, d * BLK : (d + 1) * BLK] = block[:, BLK:]
    copies = [
        pltpu.make_async_copy(rows_ref.at[0], x_hbm, sems.at[3]),
        pltpu.make_async_copy(rows_ref.at[1], dy_hbm, sems.at[4]),
    ]
    for k in range(3):
        rows = rows_ref[k // 2]
        low = jnp.concatenate([w0[k], w1[k]], axis=0)
        high = jnp.concatenate([w2[k], w3[k]], axis=0)
        total = dot(rows[:, : 2 * BLK], low, ((1,), (0,))) + dot(
            rows[:, 2 * BLK :], high, ((1,), (0,))
        )
        at = slice(k * FF, (k + 1) * FF)
        sums_ref[:, at] = total.astype(BF16)
        copies.append(pltpu.make_async_copy(sums_ref.at[:, at], sums_hbm.at[:, at], sems.at[k]))
        copies[-1].start()
    copies[0].start()
    copies[1].start()
    for copy in copies:
        copy.wait()


def partial_sums(*operands):
    vmem, hbm = [pl.BlockSpec(memory_space=m) for m in (pltpu.VMEM, pltpu.HBM)]
    return pl.pallas_call(
        partial_kernel,
        out_shape=(far_shape(ROWS, 3 * FF), far_shape(ROWS, 4 * BLK), far_shape(ROWS, 4 * BLK)),
        in_specs=[vmem] * 5,
        out_specs=[hbm] * 3,
        scratch_shapes=[
            pltpu.VMEM((ROWS, 3 * FF), BF16),
            pltpu.VMEM((2, ROWS, 4 * BLK), BF16),
            pltpu.SemaphoreType.DMA((5,)),
        ],
        compiler_params=PARAMS,
        cost_estimate=pl.CostEstimate(
            flops=2 * 3 * ROWS * FF * 4 * BLK, bytes_accessed=4000000, transcendentals=0
        ),
    )(*operands)


def act_kernel(in_ref, out_ref):
    rows = ROWS // Y
    for lo in range(0, FF, 256):
        vals = []
        for k in range(3):
            block = in_ref[:, k * FF + lo : k * FF + lo + 256].astype(F32)
            total = block[:rows]
            for y in range(1, Y):
                total = total + block[y * rows : (y + 1) * rows]
            vals.append(total)
        gate, up, back = vals
        s = jax.nn.sigmoid(gate)
        act = gate * s * up
        grad_g = back * up * s * (1.0 + gate * (1.0 - s))
        grad_u = back * gate * s
        for k, value in enumerate((act, grad_g, grad_u)):
            at = slice(k * FF + lo, k * FF + lo + 256)
            out_ref[:, at] = jnp.concatenate([value] * Y, axis=0).astype(BF16)


def back_kernel(h_ref, w0, w1, w2, w3, pay_ref):
    act = h_ref[:, :FF]
    grad_g = h_ref[:, FF : 2 * FF]
    grad_u = h_ref[:, 2 * FF :]
    outputs = []
    for wa, wb in ((w0, w1), (w2, w3)):
        weights = [jnp.concatenate([wa[k], wb[k]], axis=0) for k in range(3)]
        y = dot(act, weights[2], ((1,), (1,))).astype(BF16)
        dx = dot(grad_g, weights[0], ((1,), (1,))) + dot(grad_u, weights[1], ((1,), (1,)))
        dx = dx.astype(BF16)
        for h in range(2):
            at = slice(h * BLK, (h + 1) * BLK)
            outputs.append(jnp.concatenate([y[:, at], dx[:, at]], axis=1))
    pair, member, slot = row_fields((WIDE, BLK), 0)
    source = member * ROWS + pair * PART + slot
    total = dot(equal_to(source, WIDE), jnp.concatenate(outputs, axis=0), ((1,), (0,)))
    pay_ref[...] = total.astype(BF16)


def grad_kernel(h_ref, x_ref, dy_ref, keep_ref, send_ref):
    for d in range(QUADS):
        for k in range(3):
            rows_ref = dy_ref if k == 2 else x_ref
            h_at = (FF, 2 * FF, 0)[k]
            part = dot(
                rows_ref[:, d * BLK : (d + 1) * BLK], h_ref[:, h_at : h_at + FF], ((0,), (0,))
            )
            if d % 2:
                send_ref[d // 2, k] = part.astype(BF16)
            else:
                keep_ref[d // 2, k] = part


def add_near_kernel(keep_ref, near_ref, kept_ref, passed_ref):
    for k in range(3):
        kept_ref[k] = keep_ref[0, k] + near_ref[0, k].astype(F32)
        passed_ref[k] = (keep_ref[1, k] + near_ref[1, k].astype(F32)).astype(BF16)


def add_far_kernel(kept_ref, other_ref, gate_ref, up_ref, down_ref):
    gate_ref[...] = (kept_ref[0] + other_ref[0].astype(F32)).astype(BF16)
    up_ref[...] = (kept_ref[1] + other_ref[1].astype(F32)).astype(BF16)
    down_ref[...] = (kept_ref[2] + other_ref[2].astype(F32)).T.astype(BF16)


def combine_kernel(q_ref, pay_ref, prob_ref, out_ref):
    prob = stacked(prob_ref[...], q_ref[0])
    mask = jnp.where(prob > 0.0, 1.0, 0.0).astype(BF16)
    parts = dot(jnp.concatenate(three(prob), axis=0), pay_ref[:, :BLK], ((1,), (0,)))
    size = QUADS * TOK
    mixed = (parts[:size] + parts[size : 2 * size]) + parts[2 * size :]
    grad = dot(mask, pay_ref[:, BLK:], ((1,), (0,)))
    out_ref[:, :BLK] = mixed.astype(BF16)
    out_ref[:, BLK:] = grad.astype(BF16)


def stack_kernel(a_ref, b_ref, c_ref, out_ref):
    for k, ref in enumerate((a_ref, b_ref, c_ref)):
        out_ref[k * NEXT : (k + 1) * NEXT] = ref[...]


def select_kernel(moving_ref, partner_ref, state_ref, a_ref, b_ref, c_ref):
    moving = moving_ref[0] != 0
    for k, ref in enumerate((a_ref, b_ref, c_ref)):
        rows = slice(k * NEXT, (k + 1) * NEXT)
        ref[...] = jnp.where(moving, partner_ref[rows], state_ref[rows])


def shape_of(*dims, dtype=BF16):
    return jax.ShapeDtypeStruct(dims, dtype)


def far_shape(*dims, dtype=BF16):
    return pltpu.HBM(dims, dtype)


def shards(
    tokens,
    grad_out,
    routes,
    gate_probs,
    w_gate,
    w_up,
    w_down,
    dest,
    next_master,
    next_first,
    next_second,
):
    quad = (lax.axis_index("y0") * 2 + lax.axis_index("core")).astype(jnp.int32).reshape(1)

    with jax.named_scope("tokens_to_quad"):
        shared = lax.all_to_all(
            call(
                blocks_kernel,
                far_shape(QUADS * TOK, 2 * BLK),
                (far(tokens), far(grad_out)),
                moved=200000,
            ),
            QUAD,
            split_axis=0,
            concat_axis=0,
            tiled=True,
        )

    with jax.named_scope("relocate"):
        mine_next = [v.reshape(NEXT, BLK) for v in (next_master, next_first, next_second)]
        state = call(stack_kernel, shape_of(3 * NEXT, BLK, dtype=F32), mine_next, moved=600000)
        partner = lax.ppermute(state, "x_hi", SWAP)

    with jax.named_scope("weights_to_quad"):
        w0 = jnp.stack([w_gate[0], w_up[0], w_down[0].T])
        w2 = lax.ppermute(w0, "y0", SWAP)
        w1 = lax.ppermute(w0, "core", SWAP)
        w2, partner, state = lax.optimization_barrier((w2, partner, state))
        w3 = lax.ppermute(w2, "core", SWAP)

    with jax.named_scope("dispatch"):
        prob, prob_again = call(
            table_kernel,
            (shape_of(TOK, WIDE, dtype=F32), far_shape(TOK, WIDE, dtype=F32)),
            (quad, far(routes.T), far(gate_probs.T)),
            flops=2 * TOK * TOK * WIDE,
            moved=300000,
        )
        pay = call(
            dispatch_kernel,
            shape_of(WIDE, 2 * BLK),
            (quad, prob, shared),
            flops=2 * 16 * TOK * WIDE * BLK,
            moved=800000,
        )
        got = lax.all_to_all(pay, EXPERT, split_axis=0, concat_axis=0, tiled=True)

    with jax.named_scope("partial_sums"):
        sums, x_rows, dy_rows = partial_sums(got, w0, w1, w2, w3)
        parts = lax.all_to_all(sums, SUMS, split_axis=0, concat_axis=0, tiled=True)

    with jax.named_scope("activation"):
        hidden = call(
            act_kernel, far_shape(ROWS, 3 * FF), (parts,), flops=4000000, moved=1000000
        )
        whole = lax.all_to_all(hidden, SUMS, split_axis=0, concat_axis=0, tiled=True)

    with jax.named_scope("slot_outputs"):
        back = call(
            back_kernel,
            far_shape(WIDE, 2 * BLK),
            (whole, w0, w1, w2, w3),
            flops=2 * 3 * ROWS * FF * 4 * BLK,
            moved=4000000,
        )
        back, whole = lax.optimization_barrier((back, whole))
        returned = lax.all_to_all(back, EXPERT, split_axis=0, concat_axis=0, tiled=True)

    with jax.named_scope("relocate"):
        moving = (dest != lax.axis_index(EXPERT).astype(jnp.int32)).astype(jnp.int32)
        moved = call(
            select_kernel,
            [far_shape(NEXT, BLK, dtype=F32)] * 3,
            (moving, partner, state),
            moved=1200000,
        )

    with jax.named_scope("weight_grads"):
        keep, send = call(
            grad_kernel,
            (shape_of(2, 3, BLK, FF, dtype=F32), shape_of(2, 3, BLK, FF)),
            (whole, x_rows, dy_rows),
            flops=40 * 3 * ROWS * FF * 4 * BLK,
            moved=100000000,
        )
        near_part = lax.ppermute(send, "core", SWAP)
        kept, passed = call(
            add_near_kernel,
            (far_shape(3, BLK, FF, dtype=F32), shape_of(3, BLK, FF)),
            (keep, near_part),
        )
        passed, moved = lax.optimization_barrier((passed, moved))
        other = lax.ppermute(passed, "y0", SWAP)
        grads = call(
            add_far_kernel,
            (far_shape(BLK, FF), far_shape(BLK, FF), far_shape(FF, BLK)),
            (kept, other),
            flops=300000,
            moved=3000000,
        )

    with jax.named_scope("combine"):
        mixes = call(
            combine_kernel,
            far_shape(QUADS * TOK, 2 * BLK),
            (quad, returned, far(prob_again)),
            flops=2 * 16 * TOK * WIDE * BLK,
            moved=800000,
        )
        mixes = lax.all_to_all(mixes, QUAD, split_axis=0, concat_axis=0, tiled=True)
        mixes = jnp.sum(mixes.reshape(QUADS, TOK, 2 * BLK).astype(F32), axis=0).astype(BF16)
        mixed, token_grad = mixes[:, :BLK], mixes[:, BLK:]

    return (
        mixed,
        token_grad,
        grads[0][None],
        grads[1][None],
        grads[2][None],
        *[v.reshape(next_master.shape) for v in moved],
    )


def solution(mesh):
    fine = Mesh(
        mesh.devices.reshape(2, 4, 2, 2, 2, 16), ("x_lo", "y1", "y0", "core", "x_hi", "z")
    )
    return jax.shard_map(
        shards,
        mesh=fine,
        in_specs=(
            P(EXPERT, DP),
            P(EXPERT, DP),
            P(EXPERT, None),
            P(EXPERT, None),
            P(EXPERT, DP, None),
            P(EXPERT, DP, None),
            P(EXPERT, None, DP),
            P(EXPERT),
            P(EXPERT, DP, None),
            P(EXPERT, DP, None),
            P(EXPERT, DP, None),
        ),
        out_specs=(
            P(EXPERT, DP),
            P(EXPERT, DP),
            P(EXPERT, DP, None),
            P(EXPERT, DP, None),
            P(EXPERT, None, DP),
            P(EXPERT, DP, None),
            P(EXPERT, DP, None),
            P(EXPERT, DP, None),
        ),
        check_vma=False,
    )
```

```python
import functools

import jax
import jax.numpy as jnp
from jax import lax
from jax.experimental import pallas as pl
from jax.experimental.pallas import tpu as pltpu
from jax.sharding import Mesh
from jax.sharding import PartitionSpec as P

EXPERT = ("x_hi", "z")
DP = ("x_lo", "y1", "y0", "core")
QUAD = ("y0", "core")
SUMS = ("x_lo", "y1")
F32 = jnp.float32
BF16 = jnp.bfloat16
SWAP = [(0, 1), (1, 0)]

TOK = 64
TOP = 8
GROUPS = 32
PART = 6
QUADS = 4
ROWS = GROUPS * PART
WIDE = GROUPS * PART * QUADS
BLK = 128
FF = 768
Y = 8
NEXT = 192

PARAMS = pltpu.CompilerParams(vmem_limit_bytes=16 * 1024 * 1024)


def far(value):
    return pltpu.with_memory_space_constraint(value, pltpu.HBM)


def call(kernel, out_shape, operands, flops=0, moved=0):
    vmem = pl.BlockSpec(memory_space=pltpu.VMEM)
    smem = pl.BlockSpec(memory_space=pltpu.SMEM)
    return pl.pallas_call(
        kernel,
        out_shape=out_shape,
        in_specs=[smem if o.dtype == jnp.int32 and o.size == 1 else vmem for o in operands],
        out_specs=jax.tree.map(lambda _: vmem, out_shape, is_leaf=lambda o: hasattr(o, "shape")),
        compiler_params=PARAMS,
        cost_estimate=pl.CostEstimate(flops=flops, bytes_accessed=moved, transcendentals=0),
    )(*operands)


def row_fields(shape, dim):
    r = lax.broadcasted_iota(jnp.int32, shape, dim)
    pair = (r * 2731) >> 16
    rest = r - pair * (QUADS * PART)
    member = (rest * 43) >> 8
    return pair, member, rest - member * PART


def three(value):
    hi = value.astype(BF16)
    left = value - hi.astype(F32)
    mid = left.astype(BF16)
    return hi, mid, (left - mid.astype(F32)).astype(BF16)


def dot(a, b, dims):
    return lax.dot_general(a, b, (dims, ((), ())), preferred_element_type=F32)


def blocks_kernel(a_ref, b_ref, out_ref):
    both = jnp.concatenate([a_ref[...], b_ref[...]], axis=1)
    for d in range(QUADS):
        out_ref[d * TOK : (d + 1) * TOK] = both


def table_kernel(q_ref, routes_ref, probs_ref, prob_ref, prob_again):
    q = q_ref[0]
    shape = (TOK, WIDE)
    pair, member, slot = row_fields(shape, 1)
    chosen = jnp.zeros(shape, F32)
    weight = jnp.zeros(shape, F32)
    expert = pair.astype(F32)
    row = lax.broadcasted_iota(jnp.int32, (TOK, TOK), 0)
    col = lax.broadcasted_iota(jnp.int32, (TOK, TOK), 1)
    unit = jnp.where(col == row, 1.0, 0.0).astype(BF16)
    routes = dot(unit, routes_ref[...].astype(F32).astype(BF16), ((1,), (1,)))
    hi, mid, low = [dot(unit, part, ((1,), (1,))) for part in three(probs_ref[...])]
    probs = (hi + mid) + low
    for k in range(TOP):
        hit = routes[:, k : k + 1] == expert
        chosen = jnp.where(hit, 1.0, chosen)
        weight = jnp.where(hit, probs[:, k : k + 1], weight)
    before = jnp.where(col < row, 1.0, 0.0).astype(BF16)
    position = dot(before, chosen.astype(BF16), ((1,), (0,)))
    here = (chosen > 0.5) & (position == (q * PART + slot).astype(F32))
    prob = jnp.where(here, weight, 0.0)
    prob_ref[...] = prob
    prob_again[...] = prob


def stacked(value, q):
    _, member, _ = row_fields(value.shape, 1)
    own = member ^ q
    return jnp.concatenate([jnp.where(own == m, value, 0.0) for m in range(QUADS)], axis=0)


def dispatch_kernel(q_ref, prob_ref, tok_ref, pay_ref):
    prob = stacked(prob_ref[...], q_ref[0])
    mask = jnp.where(prob > 0.0, 1.0, 0.0).astype(BF16)
    pay_ref[:, :BLK] = dot(mask, tok_ref[:, :BLK], ((0,), (0,))).astype(BF16)
    parts = jnp.concatenate(three(prob), axis=0)
    cotangents = jnp.concatenate([tok_ref[:, BLK:]] * 3, axis=0)
    pay_ref[:, BLK:] = dot(parts, cotangents, ((0,), (0,))).astype(BF16)


def equal_to(want, width):
    lane = lax.broadcasted_iota(jnp.int32, want.shape, 1)
    return jnp.concatenate(
        [jnp.where(want == lane + at, 1.0, 0.0).astype(BF16) for at in range(0, width, BLK)],
        axis=1,
    )


def place(d):
    i = lax.broadcasted_iota(jnp.int32, (ROWS, BLK), 0)
    group = (i * 10923) >> 16
    return equal_to(group * (QUADS * PART) + d * PART + (i - group * PART), WIDE)


def partial_kernel(pay_ref, w0, w1, w2, w3, sums_hbm, x_hbm, dy_hbm, sums_ref, rows_ref, sems):
    got = pay_ref[...]
    for d in range(QUADS):
        moved = dot(place(d), got, ((1,), (0,))).astype(BF16)
        rows_ref[0, :, d * BLK : (d + 1) * BLK] = moved[:, :BLK]
        rows_ref[1, :, d * BLK : (d + 1) * BLK] = moved[:, BLK:]
    copies = [
        pltpu.make_async_copy(rows_ref.at[0], x_hbm, sems.at[3]),
        pltpu.make_async_copy(rows_ref.at[1], dy_hbm, sems.at[4]),
    ]
    for k in range(3):
        rows = rows_ref[k // 2]
        low = jnp.concatenate([w0[k], w1[k]], axis=0)
        high = jnp.concatenate([w2[k], w3[k]], axis=0)
        total = dot(rows[:, : 2 * BLK], low, ((1,), (0,))) + dot(
            rows[:, 2 * BLK :], high, ((1,), (0,))
        )
        at = slice(k * FF, (k + 1) * FF)
        sums_ref[:, at] = total.astype(BF16)
        copies.append(pltpu.make_async_copy(sums_ref.at[:, at], sums_hbm.at[:, at], sems.at[k]))
        copies[-1].start()
    copies[0].start()
    copies[1].start()
    for copy in copies:
        copy.wait()


def partial_sums(*operands):
    vmem, hbm = [pl.BlockSpec(memory_space=m) for m in (pltpu.VMEM, pltpu.HBM)]
    return pl.pallas_call(
        partial_kernel,
        out_shape=(far_shape(ROWS, 3 * FF), far_shape(ROWS, 4 * BLK), far_shape(ROWS, 4 * BLK)),
        in_specs=[vmem] * 5,
        out_specs=[hbm] * 3,
        scratch_shapes=[
            pltpu.VMEM((ROWS, 3 * FF), BF16),
            pltpu.VMEM((2, ROWS, 4 * BLK), BF16),
            pltpu.SemaphoreType.DMA((5,)),
        ],
        compiler_params=PARAMS,
        cost_estimate=pl.CostEstimate(
            flops=2 * 3 * ROWS * FF * 4 * BLK, bytes_accessed=4000000, transcendentals=0
        ),
    )(*operands)


def act_kernel(in_ref, out_ref):
    rows = ROWS // Y
    for lo in range(0, FF, 256):
        vals = []
        for k in range(3):
            block = in_ref[:, k * FF + lo : k * FF + lo + 256].astype(F32)
            total = block[:rows]
            for y in range(1, Y):
                total = total + block[y * rows : (y + 1) * rows]
            vals.append(total)
        gate, up, back = vals
        s = jax.nn.sigmoid(gate)
        act = gate * s * up
        grad_g = back * up * s * (1.0 + gate * (1.0 - s))
        grad_u = back * gate * s
        for k, value in enumerate((act, grad_g, grad_u)):
            at = slice(k * FF + lo, k * FF + lo + 256)
            out_ref[:, at] = jnp.concatenate([value] * Y, axis=0).astype(BF16)


def back_kernel(h_ref, w0, w1, w2, w3, pay_ref):
    act = h_ref[:, :FF]
    grad_g = h_ref[:, FF : 2 * FF]
    grad_u = h_ref[:, 2 * FF :]
    outputs = []
    for wa, wb in ((w0, w1), (w2, w3)):
        weights = [jnp.concatenate([wa[k], wb[k]], axis=0) for k in range(3)]
        y = dot(act, weights[2], ((1,), (1,))).astype(BF16)
        dx = dot(grad_g, weights[0], ((1,), (1,))) + dot(grad_u, weights[1], ((1,), (1,)))
        dx = dx.astype(BF16)
        for h in range(2):
            at = slice(h * BLK, (h + 1) * BLK)
            outputs.append(jnp.concatenate([y[:, at], dx[:, at]], axis=1))
    pair, member, slot = row_fields((WIDE, BLK), 0)
    source = member * ROWS + pair * PART + slot
    total = dot(equal_to(source, WIDE), jnp.concatenate(outputs, axis=0), ((1,), (0,)))
    pay_ref[...] = total.astype(BF16)


def grad_kernel(h_ref, x_ref, dy_ref, keep_ref, send_ref):
    for d in range(QUADS):
        for k in range(3):
            rows_ref = dy_ref if k == 2 else x_ref
            h_at = (FF, 2 * FF, 0)[k]
            part = dot(
                rows_ref[:, d * BLK : (d + 1) * BLK], h_ref[:, h_at : h_at + FF], ((0,), (0,))
            )
            if d % 2:
                send_ref[d // 2, k] = part.astype(BF16)
            else:
                keep_ref[d // 2, k] = part


def add_near_kernel(keep_ref, near_ref, kept_ref, passed_ref):
    for k in range(3):
        kept_ref[k] = keep_ref[0, k] + near_ref[0, k].astype(F32)
        passed_ref[k] = (keep_ref[1, k] + near_ref[1, k].astype(F32)).astype(BF16)


def add_far_kernel(kept_ref, other_ref, gate_ref, up_ref, down_ref):
    gate_ref[...] = (kept_ref[0] + other_ref[0].astype(F32)).astype(BF16)
    up_ref[...] = (kept_ref[1] + other_ref[1].astype(F32)).astype(BF16)
    down_ref[...] = (kept_ref[2] + other_ref[2].astype(F32)).T.astype(BF16)


def combine_kernel(q_ref, pay_ref, prob_ref, out_ref):
    q = q_ref[0]
    shape = (TOK, WIDE)
    _, member, _ = row_fields(shape, 1)
    y = pay_ref[:, :BLK]
    dx = pay_ref[:, BLK:]
    prob = prob_ref[...]
    mask = jnp.where(prob > 0.0, 1.0, 0.0)
    for d in range(QUADS):
        at = member == d
        mixed = jnp.zeros((TOK, BLK), F32)
        for part in three(jnp.where(at, prob, 0.0)):
            mixed = mixed + dot(part, y, ((1,), (0,)))
        grad = dot(jnp.where(at, mask, 0.0).astype(BF16), dx, ((1,), (0,)))
        out_ref[q ^ d] = jnp.concatenate([mixed, grad], axis=1).astype(BF16)


def stack_kernel(a_ref, b_ref, c_ref, out_ref):
    for k, ref in enumerate((a_ref, b_ref, c_ref)):
        out_ref[k * NEXT : (k + 1) * NEXT] = ref[...]


def select_kernel(moving_ref, partner_ref, state_ref, a_ref, b_ref, c_ref):
    moving = moving_ref[0] != 0
    for k, ref in enumerate((a_ref, b_ref, c_ref)):
        rows = slice(k * NEXT, (k + 1) * NEXT)
        ref[...] = jnp.where(moving, partner_ref[rows], state_ref[rows])


def shape_of(*dims, dtype=BF16):
    return jax.ShapeDtypeStruct(dims, dtype)


def far_shape(*dims, dtype=BF16):
    return pltpu.HBM(dims, dtype)


def shards(
    tokens,
    grad_out,
    routes,
    gate_probs,
    w_gate,
    w_up,
    w_down,
    dest,
    next_master,
    next_first,
    next_second,
):
    quad = (lax.axis_index("y0") * 2 + lax.axis_index("core")).astype(jnp.int32).reshape(1)

    with jax.named_scope("tokens_to_quad"):
        shared = lax.all_to_all(
            call(
                blocks_kernel,
                far_shape(QUADS * TOK, 2 * BLK),
                (far(tokens), far(grad_out)),
                moved=200000,
            ),
            QUAD,
            split_axis=0,
            concat_axis=0,
            tiled=True,
        )

    with jax.named_scope("relocate"):
        mine_next = [v.reshape(NEXT, BLK) for v in (next_master, next_first, next_second)]
        state = call(stack_kernel, shape_of(3 * NEXT, BLK, dtype=F32), mine_next, moved=600000)
        partner = lax.ppermute(state, "x_hi", SWAP)

    with jax.named_scope("weights_to_quad"):
        w0 = jnp.stack([w_gate[0], w_up[0], w_down[0].T])
        w2 = lax.ppermute(w0, "y0", SWAP)
        w1 = lax.ppermute(w0, "core", SWAP)
        w2, partner, state = lax.optimization_barrier((w2, partner, state))
        w3 = lax.ppermute(w2, "core", SWAP)

    with jax.named_scope("dispatch"):
        prob, prob_again = call(
            table_kernel,
            (shape_of(TOK, WIDE, dtype=F32), far_shape(TOK, WIDE, dtype=F32)),
            (quad, far(routes.T), far(gate_probs.T)),
            flops=2 * TOK * TOK * WIDE,
            moved=300000,
        )
        pay = call(
            dispatch_kernel,
            shape_of(WIDE, 2 * BLK),
            (quad, prob, shared),
            flops=2 * 16 * TOK * WIDE * BLK,
            moved=800000,
        )
        got = lax.all_to_all(pay, EXPERT, split_axis=0, concat_axis=0, tiled=True)

    with jax.named_scope("partial_sums"):
        sums, x_rows, dy_rows = partial_sums(got, w0, w1, w2, w3)
        parts = lax.all_to_all(sums, SUMS, split_axis=0, concat_axis=0, tiled=True)

    with jax.named_scope("activation"):
        hidden = call(
            act_kernel, far_shape(ROWS, 3 * FF), (parts,), flops=4000000, moved=1000000
        )
        whole = lax.all_to_all(hidden, SUMS, split_axis=0, concat_axis=0, tiled=True)

    with jax.named_scope("slot_outputs"):
        back = call(
            back_kernel,
            far_shape(WIDE, 2 * BLK),
            (whole, w0, w1, w2, w3),
            flops=2 * 3 * ROWS * FF * 4 * BLK,
            moved=4000000,
        )
        back, whole = lax.optimization_barrier((back, whole))
        returned = lax.all_to_all(back, EXPERT, split_axis=0, concat_axis=0, tiled=True)

    with jax.named_scope("relocate"):
        moving = (dest != lax.axis_index(EXPERT).astype(jnp.int32)).astype(jnp.int32)
        moved = call(
            select_kernel,
            [far_shape(NEXT, BLK, dtype=F32)] * 3,
            (moving, partner, state),
            moved=1200000,
        )

    with jax.named_scope("weight_grads"):
        keep, send = call(
            grad_kernel,
            (shape_of(2, 3, BLK, FF, dtype=F32), shape_of(2, 3, BLK, FF)),
            (whole, x_rows, dy_rows),
            flops=40 * 3 * ROWS * FF * 4 * BLK,
            moved=100000000,
        )
        near_part = lax.ppermute(send, "core", SWAP)
        kept, passed = call(
            add_near_kernel,
            (far_shape(3, BLK, FF, dtype=F32), shape_of(3, BLK, FF)),
            (keep, near_part),
        )
        passed, moved = lax.optimization_barrier((passed, moved))
        other = lax.ppermute(passed, "y0", SWAP)
        grads = call(
            add_far_kernel,
            (far_shape(BLK, FF), far_shape(BLK, FF), far_shape(FF, BLK)),
            (kept, other),
            flops=300000,
            moved=3000000,
        )

    with jax.named_scope("combine"):
        mixes = call(
            combine_kernel,
            shape_of(QUADS, TOK, 2 * BLK),
            (quad, returned, far(prob_again)),
            flops=2 * 16 * TOK * WIDE * BLK,
            moved=800000,
        )
        mixes = lax.all_to_all(mixes, QUAD, split_axis=0, concat_axis=0, tiled=True)
        mixes = jnp.sum(mixes.astype(F32), axis=0).astype(BF16)
        mixed, token_grad = mixes[:, :BLK], mixes[:, BLK:]

    return (
        mixed,
        token_grad,
        grads[0][None],
        grads[1][None],
        grads[2][None],
        *[v.reshape(next_master.shape) for v in moved],
    )


def solution(mesh):
    fine = Mesh(
        mesh.devices.reshape(2, 4, 2, 2, 2, 16), ("x_lo", "y1", "y0", "core", "x_hi", "z")
    )
    return jax.shard_map(
        shards,
        mesh=fine,
        in_specs=(
            P(EXPERT, DP),
            P(EXPERT, DP),
            P(EXPERT, None),
            P(EXPERT, None),
            P(EXPERT, DP, None),
            P(EXPERT, DP, None),
            P(EXPERT, None, DP),
            P(EXPERT),
            P(EXPERT, DP, None),
            P(EXPERT, DP, None),
            P(EXPERT, DP, None),
        ),
        out_specs=(
            P(EXPERT, DP),
            P(EXPERT, DP),
            P(EXPERT, DP, None),
            P(EXPERT, DP, None),
            P(EXPERT, None, DP),
            P(EXPERT, DP, None),
            P(EXPERT, DP, None),
            P(EXPERT, DP, None),
        ),
        check_vma=False,
    )
```

```python
import functools

import jax
import jax.numpy as jnp
from jax import lax
from jax.experimental import pallas as pl
from jax.experimental.pallas import tpu as pltpu
from jax.sharding import Mesh
from jax.sharding import PartitionSpec as P

EXPERT = ("x_hi", "z")
DP = ("x_lo", "y1", "y0", "core")
QUAD = ("y0", "core")
SUMS = ("y1", "x_lo")
F32 = jnp.float32
BF16 = jnp.bfloat16
SWAP = [(0, 1), (1, 0)]

TOK = 64
TOP = 8
GROUPS = 32
PART = 6
QUADS = 4
ROWS = GROUPS * PART
WIDE = GROUPS * PART * QUADS
BLK = 128
FF = 768
Y = 8
NEXT = 192

PARAMS = pltpu.CompilerParams(vmem_limit_bytes=16 * 1024 * 1024)


def far(value):
    return pltpu.with_memory_space_constraint(value, pltpu.HBM)


def call(kernel, out_shape, operands, flops=0, moved=0):
    vmem = pl.BlockSpec(memory_space=pltpu.VMEM)
    smem = pl.BlockSpec(memory_space=pltpu.SMEM)
    return pl.pallas_call(
        kernel,
        out_shape=out_shape,
        in_specs=[smem if o.dtype == jnp.int32 and o.size == 1 else vmem for o in operands],
        out_specs=jax.tree.map(lambda _: vmem, out_shape, is_leaf=lambda o: hasattr(o, "shape")),
        compiler_params=PARAMS,
        cost_estimate=pl.CostEstimate(flops=flops, bytes_accessed=moved, transcendentals=0),
    )(*operands)


def row_fields(shape, dim):
    r = lax.broadcasted_iota(jnp.int32, shape, dim)
    pair = (r * 2731) >> 16
    rest = r - pair * (QUADS * PART)
    member = (rest * 43) >> 8
    return pair, member, rest - member * PART


def three(value):
    hi = value.astype(BF16)
    left = value - hi.astype(F32)
    mid = left.astype(BF16)
    return hi, mid, (left - mid.astype(F32)).astype(BF16)


def dot(a, b, dims):
    return lax.dot_general(a, b, (dims, ((), ())), preferred_element_type=F32)


def blocks_kernel(a_ref, b_ref, out_ref):
    both = jnp.concatenate([a_ref[...], b_ref[...]], axis=1)
    for d in range(QUADS):
        out_ref[d * TOK : (d + 1) * TOK] = both


def table_kernel(q_ref, routes_ref, probs_ref, prob_ref, prob_again):
    q = q_ref[0]
    shape = (TOK, WIDE)
    pair, member, slot = row_fields(shape, 1)
    chosen = jnp.zeros(shape, F32)
    weight = jnp.zeros(shape, F32)
    expert = pair.astype(F32)
    row = lax.broadcasted_iota(jnp.int32, (TOK, TOK), 0)
    col = lax.broadcasted_iota(jnp.int32, (TOK, TOK), 1)
    unit = jnp.where(col == row, 1.0, 0.0).astype(BF16)
    routes = dot(unit, routes_ref[...].astype(F32).astype(BF16), ((1,), (1,)))
    hi, mid, low = [dot(unit, part, ((1,), (1,))) for part in three(probs_ref[...])]
    probs = (hi + mid) + low
    for k in range(TOP):
        hit = routes[:, k : k + 1] == expert
        chosen = jnp.where(hit, 1.0, chosen)
        weight = jnp.where(hit, probs[:, k : k + 1], weight)
    before = jnp.where(col < row, 1.0, 0.0).astype(BF16)
    position = dot(before, chosen.astype(BF16), ((1,), (0,)))
    here = (chosen > 0.5) & (position == (q * PART + slot).astype(F32))
    prob = jnp.where(here, weight, 0.0)
    prob_ref[...] = prob
    prob_again[...] = prob


def stacked(value, q):
    _, member, _ = row_fields(value.shape, 1)
    own = member ^ q
    return jnp.concatenate([jnp.where(own == m, value, 0.0) for m in range(QUADS)], axis=0)


def dispatch_kernel(q_ref, prob_ref, tok_ref, pay_ref):
    prob = stacked(prob_ref[...], q_ref[0])
    mask = jnp.where(prob > 0.0, 1.0, 0.0).astype(BF16)
    pay_ref[:, :BLK] = dot(mask, tok_ref[:, :BLK], ((0,), (0,))).astype(BF16)
    parts = jnp.concatenate(three(prob), axis=0)
    cotangents = jnp.concatenate([tok_ref[:, BLK:]] * 3, axis=0)
    pay_ref[:, BLK:] = dot(parts, cotangents, ((0,), (0,))).astype(BF16)


def equal_to(want, width):
    lane = lax.broadcasted_iota(jnp.int32, want.shape, 1)
    return jnp.concatenate(
        [jnp.where(want == lane + at, 1.0, 0.0).astype(BF16) for at in range(0, width, BLK)],
        axis=1,
    )


def place(d):
    i = lax.broadcasted_iota(jnp.int32, (ROWS, BLK), 0)
    group = (i * 10923) >> 16
    return equal_to(group * (QUADS * PART) + d * PART + (i - group * PART), WIDE)


def partial_kernel(pay_ref, w0, w1, w2, w3, sums_hbm, x_hbm, dy_hbm, sums_ref, rows_ref, sems):
    got = pay_ref[...]
    for d in range(QUADS):
        moved = dot(place(d), got, ((1,), (0,))).astype(BF16)
        rows_ref[0, :, d * BLK : (d + 1) * BLK] = moved[:, :BLK]
        rows_ref[1, :, d * BLK : (d + 1) * BLK] = moved[:, BLK:]
    copies = [
        pltpu.make_async_copy(rows_ref.at[0], x_hbm, sems.at[3]),
        pltpu.make_async_copy(rows_ref.at[1], dy_hbm, sems.at[4]),
    ]
    for k in range(3):
        rows = rows_ref[k // 2]
        low = jnp.concatenate([w0[k], w1[k]], axis=0)
        high = jnp.concatenate([w2[k], w3[k]], axis=0)
        total = dot(rows[:, : 2 * BLK], low, ((1,), (0,))) + dot(
            rows[:, 2 * BLK :], high, ((1,), (0,))
        )
        at = slice(k * FF, (k + 1) * FF)
        sums_ref[:, at] = total.astype(BF16)
        copies.append(pltpu.make_async_copy(sums_ref.at[:, at], sums_hbm.at[:, at], sems.at[k]))
        copies[-1].start()
    copies[0].start()
    copies[1].start()
    for copy in copies:
        copy.wait()


def partial_sums(*operands):
    vmem, hbm = [pl.BlockSpec(memory_space=m) for m in (pltpu.VMEM, pltpu.HBM)]
    return pl.pallas_call(
        partial_kernel,
        out_shape=(far_shape(ROWS, 3 * FF), far_shape(ROWS, 4 * BLK), far_shape(ROWS, 4 * BLK)),
        in_specs=[vmem] * 5,
        out_specs=[hbm] * 3,
        scratch_shapes=[
            pltpu.VMEM((ROWS, 3 * FF), BF16),
            pltpu.VMEM((2, ROWS, 4 * BLK), BF16),
            pltpu.SemaphoreType.DMA((5,)),
        ],
        compiler_params=PARAMS,
        cost_estimate=pl.CostEstimate(
            flops=2 * 3 * ROWS * FF * 4 * BLK, bytes_accessed=4000000, transcendentals=0
        ),
    )(*operands)


def act_kernel(in_ref, out_ref):
    rows = ROWS // Y
    for lo in range(0, FF, 256):
        vals = []
        for k in range(3):
            block = in_ref[:, k * FF + lo : k * FF + lo + 256].astype(F32)
            total = block[:rows]
            for y in range(1, Y):
                total = total + block[y * rows : (y + 1) * rows]
            vals.append(total)
        gate, up, back = vals
        s = jax.nn.sigmoid(gate)
        act = gate * s * up
        grad_g = back * up * s * (1.0 + gate * (1.0 - s))
        grad_u = back * gate * s
        for k, value in enumerate((act, grad_g, grad_u)):
            at = slice(k * FF + lo, k * FF + lo + 256)
            out_ref[:, at] = jnp.concatenate([value] * Y, axis=0).astype(BF16)


def back_kernel(h_ref, w0, w1, w2, w3, pay_ref):
    act = h_ref[:, :FF]
    grad_g = h_ref[:, FF : 2 * FF]
    grad_u = h_ref[:, 2 * FF :]
    outputs = []
    for wa, wb in ((w0, w1), (w2, w3)):
        weights = [jnp.concatenate([wa[k], wb[k]], axis=0) for k in range(3)]
        y = dot(act, weights[2], ((1,), (1,))).astype(BF16)
        dx = dot(grad_g, weights[0], ((1,), (1,))) + dot(grad_u, weights[1], ((1,), (1,)))
        dx = dx.astype(BF16)
        for h in range(2):
            at = slice(h * BLK, (h + 1) * BLK)
            outputs.append(jnp.concatenate([y[:, at], dx[:, at]], axis=1))
    pair, member, slot = row_fields((WIDE, BLK), 0)
    source = member * ROWS + pair * PART + slot
    total = dot(equal_to(source, WIDE), jnp.concatenate(outputs, axis=0), ((1,), (0,)))
    pay_ref[...] = total.astype(BF16)


def grad_kernel(h_ref, x_ref, dy_ref, keep_ref, send_ref):
    for d in range(QUADS):
        for k in range(3):
            rows_ref = dy_ref if k == 2 else x_ref
            h_at = (FF, 2 * FF, 0)[k]
            part = dot(
                rows_ref[:, d * BLK : (d + 1) * BLK], h_ref[:, h_at : h_at + FF], ((0,), (0,))
            )
            if d % 2:
                send_ref[d // 2, k] = part.astype(BF16)
            else:
                keep_ref[d // 2, k] = part


def add_near_kernel(keep_ref, near_ref, kept_ref, passed_ref):
    for k in range(3):
        kept_ref[k] = keep_ref[0, k] + near_ref[0, k].astype(F32)
        passed_ref[k] = (keep_ref[1, k] + near_ref[1, k].astype(F32)).astype(BF16)


def add_far_kernel(kept_ref, other_ref, gate_ref, up_ref, down_ref):
    gate_ref[...] = (kept_ref[0] + other_ref[0].astype(F32)).astype(BF16)
    up_ref[...] = (kept_ref[1] + other_ref[1].astype(F32)).astype(BF16)
    down_ref[...] = (kept_ref[2] + other_ref[2].astype(F32)).T.astype(BF16)


def combine_kernel(q_ref, pay_ref, prob_ref, out_ref):
    q = q_ref[0]
    shape = (TOK, WIDE)
    _, member, _ = row_fields(shape, 1)
    y = pay_ref[:, :BLK]
    dx = pay_ref[:, BLK:]
    prob = prob_ref[...]
    mask = jnp.where(prob > 0.0, 1.0, 0.0)
    for d in range(QUADS):
        at = member == d
        mixed = jnp.zeros((TOK, BLK), F32)
        for part in three(jnp.where(at, prob, 0.0)):
            mixed = mixed + dot(part, y, ((1,), (0,)))
        grad = dot(jnp.where(at, mask, 0.0).astype(BF16), dx, ((1,), (0,)))
        out_ref[q ^ d] = jnp.concatenate([mixed, grad], axis=1).astype(BF16)


def stack_kernel(a_ref, b_ref, c_ref, out_ref):
    for k, ref in enumerate((a_ref, b_ref, c_ref)):
        out_ref[k * NEXT : (k + 1) * NEXT] = ref[...]


def select_kernel(moving_ref, partner_ref, state_ref, a_ref, b_ref, c_ref):
    moving = moving_ref[0] != 0
    for k, ref in enumerate((a_ref, b_ref, c_ref)):
        rows = slice(k * NEXT, (k + 1) * NEXT)
        ref[...] = jnp.where(moving, partner_ref[rows], state_ref[rows])


def shape_of(*dims, dtype=BF16):
    return jax.ShapeDtypeStruct(dims, dtype)


def far_shape(*dims, dtype=BF16):
    return pltpu.HBM(dims, dtype)


def shards(
    tokens,
    grad_out,
    routes,
    gate_probs,
    w_gate,
    w_up,
    w_down,
    dest,
    next_master,
    next_first,
    next_second,
):
    quad = (lax.axis_index("y0") * 2 + lax.axis_index("core")).astype(jnp.int32).reshape(1)

    with jax.named_scope("tokens_to_quad"):
        shared = lax.all_to_all(
            call(
                blocks_kernel,
                far_shape(QUADS * TOK, 2 * BLK),
                (far(tokens), far(grad_out)),
                moved=200000,
            ),
            QUAD,
            split_axis=0,
            concat_axis=0,
            tiled=True,
        )

    with jax.named_scope("relocate"):
        mine_next = [v.reshape(NEXT, BLK) for v in (next_master, next_first, next_second)]
        state = call(stack_kernel, shape_of(3 * NEXT, BLK, dtype=F32), mine_next, moved=600000)
        partner = lax.ppermute(state, "x_hi", SWAP)

    with jax.named_scope("weights_to_quad"):
        w0 = jnp.stack([w_gate[0], w_up[0], w_down[0].T])
        w2 = lax.ppermute(w0, "y0", SWAP)
        w1 = lax.ppermute(w0, "core", SWAP)
        w2, partner, state = lax.optimization_barrier((w2, partner, state))
        w3 = lax.ppermute(w2, "core", SWAP)

    with jax.named_scope("dispatch"):
        prob, prob_again = call(
            table_kernel,
            (shape_of(TOK, WIDE, dtype=F32), far_shape(TOK, WIDE, dtype=F32)),
            (quad, far(routes.T), far(gate_probs.T)),
            flops=2 * TOK * TOK * WIDE,
            moved=300000,
        )
        pay = call(
            dispatch_kernel,
            shape_of(WIDE, 2 * BLK),
            (quad, prob, shared),
            flops=2 * 16 * TOK * WIDE * BLK,
            moved=800000,
        )
        got = lax.all_to_all(pay, EXPERT, split_axis=0, concat_axis=0, tiled=True)

    with jax.named_scope("partial_sums"):
        sums, x_rows, dy_rows = partial_sums(got, w0, w1, w2, w3)
        parts = lax.all_to_all(sums, SUMS, split_axis=0, concat_axis=0, tiled=True)

    with jax.named_scope("activation"):
        hidden = call(
            act_kernel, far_shape(ROWS, 3 * FF), (parts,), flops=4000000, moved=1000000
        )
        whole = lax.all_to_all(hidden, SUMS, split_axis=0, concat_axis=0, tiled=True)

    with jax.named_scope("slot_outputs"):
        back = call(
            back_kernel,
            far_shape(WIDE, 2 * BLK),
            (whole, w0, w1, w2, w3),
            flops=2 * 3 * ROWS * FF * 4 * BLK,
            moved=4000000,
        )
        back, whole = lax.optimization_barrier((back, whole))
        returned = lax.all_to_all(back, EXPERT, split_axis=0, concat_axis=0, tiled=True)

    with jax.named_scope("relocate"):
        moving = (dest != lax.axis_index(EXPERT).astype(jnp.int32)).astype(jnp.int32)
        moved = call(
            select_kernel,
            [far_shape(NEXT, BLK, dtype=F32)] * 3,
            (moving, partner, state),
            moved=1200000,
        )

    with jax.named_scope("weight_grads"):
        keep, send = call(
            grad_kernel,
            (shape_of(2, 3, BLK, FF, dtype=F32), shape_of(2, 3, BLK, FF)),
            (whole, x_rows, dy_rows),
            flops=40 * 3 * ROWS * FF * 4 * BLK,
            moved=100000000,
        )
        near_part = lax.ppermute(send, "core", SWAP)
        kept, passed = call(
            add_near_kernel,
            (far_shape(3, BLK, FF, dtype=F32), shape_of(3, BLK, FF)),
            (keep, near_part),
        )
        passed, moved = lax.optimization_barrier((passed, moved))
        other = lax.ppermute(passed, "y0", SWAP)
        grads = call(
            add_far_kernel,
            (far_shape(BLK, FF), far_shape(BLK, FF), far_shape(FF, BLK)),
            (kept, other),
            flops=300000,
            moved=3000000,
        )

    with jax.named_scope("combine"):
        mixes = call(
            combine_kernel,
            shape_of(QUADS, TOK, 2 * BLK),
            (quad, returned, far(prob_again)),
            flops=2 * 16 * TOK * WIDE * BLK,
            moved=800000,
        )
        mixes = lax.all_to_all(mixes, QUAD, split_axis=0, concat_axis=0, tiled=True)
        mixes = jnp.sum(mixes.astype(F32), axis=0).astype(BF16)
        mixed, token_grad = mixes[:, :BLK], mixes[:, BLK:]

    return (
        mixed,
        token_grad,
        grads[0][None],
        grads[1][None],
        grads[2][None],
        *[v.reshape(next_master.shape) for v in moved],
    )


def solution(mesh):
    fine = Mesh(
        mesh.devices.reshape(2, 4, 2, 2, 2, 16), ("x_lo", "y1", "y0", "core", "x_hi", "z")
    )
    return jax.shard_map(
        shards,
        mesh=fine,
        in_specs=(
            P(EXPERT, DP),
            P(EXPERT, DP),
            P(EXPERT, None),
            P(EXPERT, None),
            P(EXPERT, DP, None),
            P(EXPERT, DP, None),
            P(EXPERT, None, DP),
            P(EXPERT),
            P(EXPERT, DP, None),
            P(EXPERT, DP, None),
            P(EXPERT, DP, None),
        ),
        out_specs=(
            P(EXPERT, DP),
            P(EXPERT, DP),
            P(EXPERT, DP, None),
            P(EXPERT, DP, None),
            P(EXPERT, None, DP),
            P(EXPERT, DP, None),
            P(EXPERT, DP, None),
            P(EXPERT, DP, None),
        ),
        check_vma=False,
    )
```
